256 devices in a mesh: inst: 32 (over x, y, core), tp: 8 (over z).
Axes of the slice: x: 4, y: 4, z: 8, core: 2. Of those that a mesh axis runs over, the one named last changes fastest.
Arguments:
- queries: bfloat16 [256, 4, 64, 128], P('inst', None, 'tp'), may hold values from -32 to 32
- new_kv: bfloat16 [256, 2, 4, 8, 128], P('inst', None, None, 'tp'), may hold values from -6 to 6
- kv_cache: bfloat16 [2048, 2, 8, 64, 128], P('inst', None, 'tp'), may hold values from -32 to 32
- block_owner: int32 [2048], P('inst'), may hold values from 0 to 255
- block_fill: int32 [2048], P('inst'), may hold values from 0 to 64, as said below
- move_slot: int32 [768], P('inst'), may hold values from 0 to 63, as said below
- move_target: int32 [768, 1], P('inst'), may hold values from 0 to 31; in each aligned block of 24 rows (0 to 23, 24 to 47, ...) at most 2 rows name the same one
- out_weight: bfloat16 [8192, 4096], P('tp'), may hold values from -0.0625 to 0.0625
Outputs:
- attention_out: bfloat16 [1024, 4096], P('inst', 'tp')
- moved_blocks: bfloat16 [2048, 2, 8, 64, 128], P('inst', None, 'tp')
The draws below stay inside these ranges and needn't reach their ends.
Inputs may be any that keep to these rules, and one draw needn't show every extreme that they name: `block_fill`: 0 marks an empty slot; the first slot of every instance is full. `move_slot`: the 24 entries of one instance name distinct slots of that instance. `move_target`: among one instance's 24 entries no destination is named more than 2 times, a bound that some block reaches.
All inputs are finite; a program needn't handle non-finite values.
Results may differ from the reference program's by a relative error of at most 0.019.
Values may be sent and summed in bfloat16 or wider, within the bound.
A program may use at most 128 MiB of HBM per device.

```python
import math
import jax
import jax.numpy as jnp
import numpy as np
from jax import lax

Q_HEADS = 64
KV_HEADS = 8
HEAD_DIM = 128
OUT_COLS = 4096
DRAFTS = 4
BLOCK_ROWS = 64
CAPACITY = 2
BLOCK_SLOTS = 64
REQUESTS = 256
INSTANCES = 32
BLOCKS = 2048
MOVE_COUNT = 24
MOVE_LIST = 768
MOVED_SLOTS = 2048


def draw_kv_cache(key, part):
    key = jax.random.fold_in(key, 1)
    base = jax.random.normal(key, (BLOCKS, 2, KV_HEADS, BLOCK_ROWS, HEAD_DIM), jnp.float32)
    values = base
    return jnp.clip(values, -32.0, 32.0).astype(jnp.bfloat16)


def draw_queries(key, part):
    key = jax.random.fold_in(key, 2)
    base = jax.random.normal(key, (REQUESTS, DRAFTS, Q_HEADS, HEAD_DIM), jnp.float32)
    values = base
    return jnp.clip(values, -32.0, 32.0).astype(jnp.bfloat16)


def draw_block_fill(key, part):
    key = jax.random.fold_in(key, 4)
    level_key, full_key, pick_key, fill_key = jax.random.split(key, 4)
    level = jax.random.randint(level_key, (INSTANCES, 1), 1, 9)
    busiest = jax.random.randint(full_key, (), 0, INSTANCES)
    level = jnp.where(jnp.arange(INSTANCES)[:, None] == busiest, 8, level)
    picked = jax.random.randint(pick_key, (INSTANCES, BLOCK_SLOTS), 0, 64)
    rows_used = jnp.minimum(jax.random.randint(fill_key, (INSTANCES, BLOCK_SLOTS), 1, 2 * BLOCK_ROWS), BLOCK_ROWS)
    first = jnp.arange(BLOCK_SLOTS)[None, :] == 0
    live = (picked < level * level) | first
    rows_used = jnp.where(first, BLOCK_ROWS, rows_used)
    return jnp.where(live, rows_used, 0).reshape(BLOCKS).astype(jnp.int32)


def draw_move_slot(key, part):
    key = jax.random.fold_in(key, 5)
    keys = jax.random.split(key, INSTANCES)
    picks = jax.vmap(lambda single: jax.random.permutation(single, BLOCK_SLOTS)[:MOVE_COUNT])(keys)
    return picks.reshape(MOVE_LIST).astype(jnp.int32)


def place_ends(drawn, rng, smallest, largest):
    index_at = [jax.random.randint(jax.random.fold_in(rng, axis), (), 0, length) for axis, length in enumerate(drawn.shape)]
    widest = drawn.shape.index(max(drawn.shape))
    beside = index_at[:widest] + [(index_at[widest] + 1) % drawn.shape[widest]] + index_at[widest + 1:]
    return drawn.at[tuple(index_at)].set(smallest).at[tuple(beside)].set(largest)


def level_of(key, dims, cuts, low, top_value):
    factor_of = 1.0
    for dim, blocks in cuts:
        heights = jax.random.uniform(jax.random.fold_in(jax.random.fold_in(key, 6), dim), (blocks,), jnp.float32, low / len(cuts), top_value / len(cuts))
        factor_of = factor_of * jnp.repeat(jnp.exp(heights), dims[dim] // blocks).reshape((-1,) + (1,) * (len(dims) - 1 - dim))
    return factor_of


def rank_table(amount, skew):
    weights = [(1 << 20) // math.isqrt(standing ** skew) + 1 for standing in range(1, amount + 1)]
    scale = 1 + sum(weights) // (1 << 30)
    return np.cumsum(np.array([max(1, weight // scale) for weight in weights]))


def skewed_ids(stream_key, shape, amount, slope):
    listing = rank_table(amount, slope)
    pick = jax.random.randint(jax.random.fold_in(stream_key, 1), shape, 0, int(listing[amount - 1]))
    grade = jnp.searchsorted(jnp.asarray(listing, jnp.int32), pick, side="right")
    return jax.random.permutation(jax.random.fold_in(stream_key, 2), amount)[grade].astype(jnp.int32)


def shared_out(stream_key, own, number, rows, number_of, top, most, skew):
    order = jax.random.permutation(stream_key, number_of)
    crowded, usual = portions_of(number_of, rows * top, most, skew, True), portions_of(number_of, rows * top, most, skew, False)
    places = jnp.arange(number_of)

    def named(tallies, offset_by):
        used = int((tallies > 0).sum())
        fixed = max(1, used // 4)
        moved = fixed + (places - fixed + offset_by * (used - fixed)) % max(1, number_of - fixed)
        return jnp.zeros((number_of,), jnp.int32).at[order[jnp.where(places < fixed, places, moved)]].set(jnp.asarray(tallies, jnp.int32))

    tallies = jnp.where(number % 4 == 0, named(crowded, number // 4), named(usual, number - number // 4 - 1))
    mixed = jax.random.permutation(jax.random.fold_in(own, 3), number_of)
    giver, receiver = mixed[0:number_of // 2 * 2:2], mixed[1:number_of // 2 * 2:2]
    margin = jnp.minimum(tallies[giver] - 1, most - tallies[receiver]) // 2
    margin = jnp.where((giver == order[0]) | (receiver == order[0]) | (tallies[receiver] == 0), 0, jnp.maximum(margin, 0))
    moved = jax.random.randint(jax.random.fold_in(own, 4), (number_of // 2,), 0, 1 << 20) % (margin + 1)
    tallies = tallies.at[giver].add(-moved).at[receiver].add(moved)
    labels = jnp.searchsorted(jnp.cumsum(tallies), jnp.arange(rows * top), side="right").astype(jnp.int32)
    table = labels.reshape(top, rows).T
    table = table[jax.random.permutation(jax.random.fold_in(own, 1), rows)]
    offset_by = jax.random.randint(jax.random.fold_in(own, 2), (rows, 1), 0, top)
    return jnp.take_along_axis(table, (jnp.arange(top)[None, :] + offset_by) % top, axis=1)


def portions_of(number_of, total, most, slope, full):
    portions = [(1 << 20) // math.isqrt(grade ** slope) + 1 for grade in range(1, number_of + 1)]
    largest = most if full else min(most, max(-(-total // number_of), total * portions[0] // sum(portions)))
    least = 1 if total - largest >= number_of - 1 else 0
    given, spare = [largest] + [least] * (number_of - 1), total - largest - least * (number_of - 1)
    while spare > 0:
        free = [i for i in range(1, number_of) if given[i] < largest] or [i for i in range(1, number_of) if given[i] < most]
        pool, budget = sum([portions[i] for i in free]), spare
        for i in free:
            addition = min(most - given[i], max(1, budget * portions[i] // pool), spare)
            given[i] = given[i] + addition
            spare = spare - addition
    return np.array(given)


def centred(rng, extent, spread, most, pieces=(), kind=jnp.bfloat16):
    result = spread * jax.random.normal(rng, extent, jnp.float32)
    if pieces:
        result = result * level_of(rng, extent, pieces, -0.22, 0.18)
    return jnp.clip(result, -most, most).astype(kind)


def setup_inputs(seed: int = 0) -> dict:
    arg_keys = jax.random.split(jax.random.key(seed), 9)
    queries = draw_queries(jax.random.fold_in(arg_keys[8], 71), 0)
    new_kv = centred(arg_keys[1], (REQUESTS, 2, DRAFTS, KV_HEADS, HEAD_DIM), 1.0, 6.0, ((0, 32), (3, 8)))
    kv_cache = draw_kv_cache(jax.random.fold_in(arg_keys[8], 71), 0)
    block_owner = place_ends(skewed_ids(arg_keys[3], (BLOCKS,), REQUESTS, 2), jax.random.fold_in(arg_keys[3], 3), 0, REQUESTS - 1).astype(jnp.int32)
    block_fill = draw_block_fill(jax.random.fold_in(arg_keys[8], 71), 0)
    move_slot = draw_move_slot(jax.random.fold_in(arg_keys[8], 71), 0)
    move_target_keys = jax.random.split(jax.random.fold_in(arg_keys[6], 1), MOVE_LIST // MOVE_COUNT)
    move_target_turns = jax.random.permutation(jax.random.fold_in(arg_keys[6], 3), MOVE_LIST // MOVE_COUNT)
    move_target = jax.vmap(lambda own, number: shared_out(jax.random.fold_in(arg_keys[6], 2), own, number, MOVE_COUNT, INSTANCES, 1, CAPACITY, 2))(move_target_keys, move_target_turns).reshape((MOVE_LIST, 1))
    out_weight = centred(arg_keys[7], (Q_HEADS * HEAD_DIM, OUT_COLS), (Q_HEADS * HEAD_DIM) ** -0.5, 0.0625, ((0, 8),))
    return dict(queries=queries, new_kv=new_kv, kv_cache=kv_cache, block_owner=block_owner, block_fill=block_fill, move_slot=move_slot, move_target=move_target, out_weight=out_weight)


MASKED = -1e30


def reference(queries, new_kv, kv_cache, block_owner, block_fill, move_slot, move_target, out_weight):
    group_size = Q_HEADS // KV_HEADS
    factor = HEAD_DIM ** -0.5
    grouped = queries.reshape(REQUESTS, DRAFTS, KV_HEADS, group_size, HEAD_DIM)
    positions = jnp.arange(BLOCK_ROWS, dtype=jnp.int32)

    def one_block(packed):
        owner, fill_rows, block = packed
        query_rows = lax.dynamic_index_in_dim(grouped, owner.astype(jnp.int32), 0, keepdims=False).astype(jnp.float32)
        key_rows = block[0].astype(jnp.float32)
        value_rows = block[1].astype(jnp.float32)
        scores = jnp.einsum("tkgd,ksd->ktgs", query_rows, key_rows, precision=lax.Precision.HIGHEST) * factor
        usable = positions < fill_rows
        highest = jnp.max(jnp.where(usable, scores, MASKED), axis=-1)
        exp_scores = jnp.where(usable, jnp.exp(scores - highest[..., None]), 0.0)
        row_total = jnp.sum(exp_scores, axis=-1)
        rounded = lax.optimization_barrier(exp_scores.astype(jnp.bfloat16)).astype(jnp.float32)
        weighted = jnp.einsum("ktgs,ksd->ktgd", rounded, value_rows, precision=lax.Precision.HIGHEST)
        return highest.reshape(-1), row_total.reshape(-1), weighted.reshape(-1, HEAD_DIM)

    block_high, block_total, block_value = lax.map(one_block, (block_owner, block_fill, kv_cache))

    draft_keys = new_kv[:, 0].astype(jnp.float32)
    draft_values = new_kv[:, 1].astype(jnp.float32)
    draft_scores = jnp.einsum("rtkgd,rukd->rktgu", grouped.astype(jnp.float32), draft_keys, precision=lax.Precision.HIGHEST) * factor
    causal = jnp.arange(DRAFTS)[None, :] <= jnp.arange(DRAFTS)[:, None]
    causal = causal[None, None, :, None, :]
    draft_high = jnp.max(jnp.where(causal, draft_scores, MASKED), axis=-1)
    draft_exp = jnp.where(causal, jnp.exp(draft_scores - draft_high[..., None]), 0.0)
    draft_total = jnp.sum(draft_exp, axis=-1)
    draft_rounded = lax.optimization_barrier(draft_exp.astype(jnp.bfloat16)).astype(jnp.float32)
    draft_value = jnp.einsum("rktgu,rukd->rktgd", draft_rounded, draft_values, precision=lax.Precision.HIGHEST)
    draft_high = draft_high.reshape(REQUESTS, -1)
    draft_total = draft_total.reshape(REQUESTS, -1)
    draft_value = draft_value.reshape(REQUESTS, -1, HEAD_DIM)

    def request_peak(owner):
        return jnp.max(jnp.where((block_owner == owner)[:, None], block_high, MASKED), axis=0)

    cache_high = lax.map(request_peak, jnp.arange(REQUESTS, dtype=jnp.int32))
    highest_all = jnp.maximum(cache_high, draft_high)
    shares = jnp.exp(block_high - highest_all[block_owner])
    draft_part = jnp.exp(draft_high - highest_all)
    numerator = jax.ops.segment_sum(shares[..., None] * block_value, block_owner, num_segments=REQUESTS)
    numerator = numerator + draft_part[..., None] * draft_value
    denominator = jax.ops.segment_sum(shares * block_total, block_owner, num_segments=REQUESTS)
    denominator = denominator + draft_part * draft_total
    attention = (numerator / denominator[..., None]).reshape(REQUESTS, KV_HEADS, DRAFTS, group_size, HEAD_DIM)
    attention = jnp.transpose(attention, (0, 2, 1, 3, 4)).reshape(REQUESTS * DRAFTS, Q_HEADS * HEAD_DIM).astype(jnp.bfloat16)
    attention_out = jnp.dot(attention, out_weight, preferred_element_type=jnp.float32).astype(jnp.bfloat16)

    target = move_target.reshape(INSTANCES, MOVE_COUNT)
    entries = jnp.arange(MOVE_COUNT, dtype=jnp.int32)
    earlier = (target[:, None, :] == target[:, :, None]) & (entries[None, None, :] < entries[None, :, None])
    arrival = jnp.sum(earlier, axis=-1).astype(jnp.int32)
    source = jnp.arange(INSTANCES, dtype=jnp.int32)[:, None]
    position = target * (INSTANCES * CAPACITY) + source * CAPACITY + arrival
    anchor = source * BLOCK_SLOTS + move_slot.reshape(INSTANCES, MOVE_COUNT)
    moved_blocks = jnp.zeros((MOVED_SLOTS, 2, KV_HEADS, BLOCK_ROWS, HEAD_DIM), jnp.bfloat16)
    moved_blocks = moved_blocks.at[position.reshape(-1).astype(jnp.int32)].set(kv_cache[anchor.reshape(-1).astype(jnp.int32)])
    return attention_out, moved_blocks
```

```python
import functools

import jax
import jax.numpy as jnp
from jax import lax
from jax.experimental import pallas as pl
from jax.experimental.pallas import tpu as pltpu
from jax.sharding import PartitionSpec as P

MESH = pl.DeviceIdType.MESH
MASKED = -1e30
CAPACITY = 2
F32, BF16, I32 = jnp.float32, jnp.bfloat16, jnp.int32

INSTS = 32
CHIPS = 16
TPS = 8
SLOTS = 64
ROWS = 64
DIM = 128
HEADS = 8
DRAFTS = 4
LINES = DRAFTS * HEADS
REQ = 8
REQS = INSTS * REQ
GROUPS = SLOTS // 4
TILES = LINES // 2
COLS = 512
MOVES = 24
EARLY = 0


def nt_dot(a, b):
    return lax.dot_general(a, b, (((1,), (1,)), ((), ())), preferred_element_type=F32)


def tile_lines(tile):
    t, g = 2 * (tile // HEADS), tile % HEADS
    return t * HEADS + g, (t + 1) * HEADS + g


def spread(weights, tile):
    first, second = tile_lines(tile)
    return jnp.concatenate(
        [
            jnp.broadcast_to(weights[:, first : first + 1], (REQ, DIM)),
            jnp.broadcast_to(weights[:, second : second + 1], (REQ, DIM)),
        ],
        axis=0,
    )


def kernel(
    q, nkv, kv_hbm, owner, fill, slot_col, target_col, target_row, w_hbm,
    out, moved,
    kv, w, pick, pick_s, msend, qall, dkv, dval, dmax, dsum,
    score, smax, ssum, reqmax, reqsum, val, pay, aux, epay, eaux, cpay, caux,
    rpay, raux, ew, acc, att, zsend, zrecv, zout,
    load_sem, own_sem, ag_s, ag_r, sib_s, sib_r, mig_s, mig_r, e_s, e_r,
    rs_s, rs_r, ra_s, ra_r, z_s, z_r,
):
    me, tp = lax.axis_index("inst"), lax.axis_index("tp")
    core = lax.rem(me, 2)
    chip = me // 2
    sibling = me ^ 1

    def remote(src, dst, send, recv, inst, z):
        return pltpu.make_async_remote_copy(
            src_ref=src, dst_ref=dst, send_sem=send, recv_sem=recv,
            device_id=(inst, z), device_id_type=MESH,
        )

    barrier = pltpu.get_barrier_semaphore()

    @pl.loop(1, INSTS)
    def _(k):
        pl.semaphore_signal(barrier, inc=1, device_id=(me ^ k, tp), device_id_type=MESH)

    @pl.loop(1, TPS)
    def _(k):
        pl.semaphore_signal(barrier, inc=1, device_id=(me, tp ^ k), device_id_type=MESH)

    kv_load = pltpu.make_async_copy(kv_hbm, kv.at[pl.ds(0, SLOTS)], load_sem.at[0])
    kv_load.start()
    w_load = pltpu.make_async_copy(w_hbm, w, load_sem.at[1])
    w_load.start()

    kv[SLOTS] = jnp.zeros((2, ROWS, DIM), BF16)
    entry_row = lax.broadcasted_iota(I32, (MOVES, MOVES), 1)
    entry_col = lax.broadcasted_iota(I32, (MOVES, MOVES), 0)
    earlier = (target_row[...] == target_col[...]) & (entry_row < entry_col)
    position = target_col[...] * CAPACITY + jnp.sum(earlier.astype(I32), axis=1, keepdims=True)
    matched = position == lax.broadcasted_iota(I32, (MOVES, DIM), 1)
    chosen = SLOTS + jnp.sum(
        jnp.where(matched, slot_col[...] - SLOTS, 0), axis=0, keepdims=True
    )
    pick[...] = jnp.broadcast_to(chosen, (8, DIM))
    pick_load = pltpu.make_async_copy(pick, pick_s, load_sem.at[2])
    pick_load.start()

    dkv[...] = jnp.zeros(dkv.shape, F32)
    dkv[:, :, 0:DRAFTS, :] = nkv[...].astype(F32)
    lane = lax.broadcasted_iota(I32, (1, DIM), 1)
    lane_group = lane // LINES

    def by_group(parts):
        return jnp.where(
            lane_group == 0,
            parts[0],
            jnp.where(lane_group == 1, parts[1], jnp.where(lane_group == 2, parts[2], parts[3])),
        )

    for half in range(REQ // 4):
        queries = q[4 * half : 4 * half + 4].reshape(4 * LINES, DIM)
        keys = dkv[4 * half : 4 * half + 4, 0].reshape(4 * 8, DIM).astype(BF16)
        full = nt_dot(keys, queries)
        scores = by_group([full[8 * i : 8 * i + 8] for i in range(4)]) * (DIM**-0.5)
        u = lax.broadcasted_iota(I32, (8, DIM), 0)
        t = lax.rem(lax.broadcasted_iota(I32, (8, DIM), 1), LINES) // HEADS
        causal = u <= t
        high = jnp.max(jnp.where(causal, scores, MASKED), axis=0, keepdims=True)
        probs = jnp.where(causal, jnp.exp(scores - high), 0.0)
        total = jnp.sum(probs, axis=0, keepdims=True)
        turned = jnp.transpose(probs).astype(BF16)
        for i in range(4):
            r = 4 * half + i
            dmax[r : r + 1, :] = high if i == 0 else pltpu.roll(high, DIM - i * LINES, 1)
            dsum[r : r + 1, :] = total if i == 0 else pltpu.roll(total, DIM - i * LINES, 1)
            dval[r * LINES : (r + 1) * LINES, :] = jnp.dot(
                turned[i * LINES : (i + 1) * LINES],
                dkv[r, 1].astype(BF16),
                preferred_element_type=F32,
            )

    qall[pl.ds(me * REQ, REQ)] = q[...]
    pl.semaphore_wait(barrier, INSTS - 1 + TPS - 1)

    def gather_in(k):
        return remote(
            q, qall.at[pl.ds(me * REQ, REQ)], ag_s.at[k], ag_r.at[k], me ^ (2 * k), tp
        )

    def gather_on(k):
        rows = pl.ds((me ^ (2 * k)) * REQ, REQ)
        return remote(qall.at[rows], qall.at[rows], sib_s.at[k], sib_r.at[k], sibling, tp)

    gather_on(0).start()

    @pl.loop(1, CHIPS)
    def _(k):
        gather_in(k).start()

    kv_load.wait()
    pick_load.wait()

    @pl.loop(0, SLOTS)
    def _(p):
        msend[p] = kv[pick_s[0, p]]

    own = pltpu.make_async_copy(
        msend.at[pl.ds(CAPACITY * me, CAPACITY)],
        moved.at[pl.ds(CAPACITY * me, CAPACITY)],
        own_sem,
    )
    own.start()

    def migrate(k):
        return remote(
            msend.at[pl.ds(CAPACITY * (me ^ k), CAPACITY)],
            moved.at[pl.ds(CAPACITY * me, CAPACITY)],
            mig_s.at[k], mig_r.at[k], me ^ k, tp,
        )

    @pl.loop(1, CHIPS)
    def _(k):
        gather_in(k).wait_recv()
        gather_on(k).start()

    @pl.loop(1, 1 + EARLY)
    def _(k):
        migrate(k).start()

    @pl.loop(0, CHIPS)
    def _(k):
        gather_on(k).wait_recv()

    row_of = lax.broadcasted_iota(I32, (ROWS, DIM), 0)

    def usable(g):
        return row_of < by_group([fill[4 * g + i] for i in range(4)])

    @pl.loop(0, GROUPS)
    def _(g):
        queries = jnp.concatenate([qall[owner[4 * g + i]] for i in range(4)], axis=0)
        keys = kv[pl.ds(4 * g, 4), 0].reshape(4 * ROWS, DIM)
        full = nt_dot(keys, queries)
        scores = by_group([full[ROWS * i : ROWS * (i + 1)] for i in range(4)]) * (DIM**-0.5)
        scores = jnp.where(usable(g), scores, MASKED)
        score[g] = scores
        smax[pl.ds(g, 1), :] = jnp.max(scores, axis=0, keepdims=True)

    row = lax.broadcasted_iota(I32, (REQS, DIM), 0)
    request = (row % (REQS // 2)) // REQ * (2 * REQ) + row // (REQS // 2) * REQ + row % REQ

    def owners(g):
        return by_group([owner[4 * g + i] for i in range(4)])

    def all_groups(x, f):
        x = f(x, pltpu.roll(x, 2 * LINES, 1))
        return f(x, pltpu.roll(x, LINES, 1))

    reqmax[...] = jnp.full(reqmax.shape, MASKED, F32)

    @pl.loop(0, GROUPS)
    def _(g):
        reqmax[...] = jnp.where(
            request == owners(g), jnp.maximum(reqmax[...], smax[pl.ds(g, 1), :]), reqmax[...]
        )

    reqmax[...] = all_groups(reqmax[...], jnp.maximum)

    @pl.loop(0, GROUPS)
    def _(g):
        highs = []
        for i in range(4):
            o = owner[4 * g + i]
            at = lax.rem(o // REQ, 2) * (REQS // 2) + o // (2 * REQ) * REQ + lax.rem(o, REQ)
            highs.append(reqmax[pl.ds(at, 1), :])
        probs = jnp.where(usable(g), jnp.exp(score[g] - by_group(highs)), 0.0)
        ssum[pl.ds(g, 1), :] = jnp.sum(probs, axis=0, keepdims=True)
        turned = jnp.transpose(probs).astype(BF16)
        for i in range(4):
            val[pl.ds((4 * g + i) * LINES, LINES), :] = jnp.dot(
                turned[i * LINES : (i + 1) * LINES],
                kv[4 * g + i, 1],
                preferred_element_type=F32,
            )

    reqsum[...] = jnp.zeros(reqsum.shape, F32)

    @pl.loop(0, GROUPS)
    def _(g):
        reqsum[...] += jnp.where(request == owners(g), ssum[pl.ds(g, 1), :], 0.0)

    reqsum[...] = all_groups(reqsum[...], jnp.add)
    aux[...] = jnp.where(lane < LINES, reqmax[...], reqsum[...]).reshape(aux.shape)

    owner_lane = lax.broadcasted_iota(I32, (1, SLOTS), 1)

    def owner_step(b, x):
        return jnp.where(owner_lane == b, owner[b], x)

    owner_row = lax.fori_loop(0, SLOTS, owner_step, jnp.zeros((1, SLOTS), I32))
    half_row = lax.broadcasted_iota(I32, (REQS // 2, SLOTS), 0)

    def sum_slots(home_core):
        ids = half_row // REQ * (2 * REQ) + home_core * REQ + half_row % REQ
        member = (ids == owner_row).astype(F32).astype(BF16)

        @pl.loop(0, TILES)
        def _(tile):
            first = 2 * HEADS * (tile // HEADS) + lax.rem(tile, HEADS)
            lines = jnp.concatenate(
                [
                    val[pl.ds(first, SLOTS, stride=LINES), :],
                    val[pl.ds(first + HEADS, SLOTS, stride=LINES), :],
                ],
                axis=1,
            ).astype(BF16)
            summed = jnp.dot(member, lines, preferred_element_type=F32)
            for c in range(CHIPS):
                both = summed[c * REQ : (c + 1) * REQ]
                pay[home_core, c, tile] = jnp.concatenate(
                    [both[:, :DIM], both[:, DIM:]], axis=0
                ).astype(BF16)

    sum_slots(1 - core)
    to_sibling = remote(pay.at[1 - core], epay, e_s.at[0], e_r.at[0], sibling, tp)
    aux_to_sibling = remote(aux.at[1 - core], eaux, e_s.at[1], e_r.at[1], sibling, tp)
    aux_to_sibling.start()
    to_sibling.start()
    sum_slots(core)
    aux_to_sibling.wait()
    to_sibling.wait()

    def join(k, into, aux_into):
        home = chip ^ k
        a, b = aux[core, home], eaux[home]
        high = jnp.maximum(a, b)
        wa, wb = jnp.exp(a - high), jnp.exp(b - high)
        total = pltpu.roll(wa, LINES, 1) * a + pltpu.roll(wb, LINES, 1) * b
        aux_into[k] = jnp.where(lane < LINES, high, total)
        for tile in range(TILES):
            into[k, tile] = (
                spread(wa, tile) * pay[core, home, tile].astype(F32)
                + spread(wb, tile) * epay[home, tile].astype(F32)
            ).astype(BF16)

    def reduce_pay(k):
        return remote(cpay.at[k], rpay.at[k], rs_s.at[k], rs_r.at[k], me ^ (2 * k), tp)

    def reduce_aux(k):
        return remote(caux.at[k], raux.at[k], ra_s.at[k], ra_r.at[k], me ^ (2 * k), tp)

    @pl.loop(0, CHIPS - 1)
    def _(i):
        k = CHIPS - 1 - i
        join(k, cpay, caux)
        reduce_aux(k).start()
        reduce_pay(k).start()

    join(0, rpay, raux)

    @pl.loop(1, CHIPS)
    def _(k):
        reduce_aux(k).wait_recv()

    def high_step(k, x):
        return jnp.maximum(x, raux[k])

    peak = lax.fori_loop(0, CHIPS, high_step, dmax[...])
    draft_weight = jnp.exp(dmax[...] - peak)

    def total_step(k, x):
        weight = jnp.exp(raux[k] - peak)
        ew[k] = weight
        return x + weight * pltpu.roll(raux[k], DIM - LINES, 1)

    total = lax.fori_loop(0, CHIPS, total_step, draft_weight * dsum[...])
    scale = 1.0 / total
    draft_weight = draft_weight * scale
    for tile in range(TILES):
        first, second = tile_lines(tile)
        acc[tile] = spread(draft_weight, tile) * jnp.concatenate(
            [dval[pl.ds(first, REQ, stride=LINES), :], dval[pl.ds(second, REQ, stride=LINES), :]],
            axis=0,
        )

    def add_source(k):
        weight = ew[k] * scale
        for tile in range(TILES):
            acc[tile] += spread(weight, tile) * rpay[k, tile].astype(F32)

    add_source(0)

    @pl.loop(1, CHIPS)
    def _(k):
        reduce_pay(k).wait_recv()
        add_source(k)

    @pl.loop(1 + EARLY, INSTS)
    def _(k):
        migrate(k).start()

    for tile in range(TILES):
        t, g = tile // HEADS, tile % HEADS
        att[t * 16 : (t + 1) * 16, g * DIM : (g + 1) * DIM] = acc[tile].astype(BF16)

    w_load.wait()

    def project(k):
        columns = pl.ds(pl.multiple_of(lax.rem(tp + k, TPS) * COLS, COLS), COLS)
        return jnp.dot(att[...], w[:, columns], preferred_element_type=F32)

    def send_columns(k):
        return remote(
            zsend.at[k], zrecv.at[k], z_s.at[k], z_r.at[k], me, lax.rem(tp + k, TPS)
        )

    @pl.loop(1, TPS)
    def _(k):
        zsend[k] = project(k).astype(BF16)
        send_columns(k).start()

    zout[...] = project(0)

    @pl.loop(1, TPS)
    def _(k):
        send_columns(k).wait_recv()
        zout[...] += zrecv[k].astype(F32)

    for t in range(DRAFTS):
        for c in range(COLS // DIM):
            zsend_rows = zout[t * REQ : (t + 1) * REQ, c * DIM : (c + 1) * DIM]
            acc_rows = pl.ds(t, REQ, stride=DRAFTS)
            dval[pl.ds(c * 32 + t, REQ, stride=DRAFTS), :] = zsend_rows
    for c in range(COLS // DIM):
        out[:, c * DIM : (c + 1) * DIM] = dval[c * 32 : (c + 1) * 32, :].astype(BF16)

    @pl.loop(1, CHIPS)
    def _(k):
        gather_in(k).wait_send()
        reduce_aux(k).wait_send()
        reduce_pay(k).wait_send()

    @pl.loop(0, CHIPS)
    def _(k):
        gather_on(k).wait_send()

    @pl.loop(1, TPS)
    def _(k):
        send_columns(k).wait_send()

    @pl.loop(1, INSTS)
    def _(k):
        migrate(k).wait()

    own.wait()


def shards(queries, new_kv, kv_cache, block_owner, block_fill, move_slot, move_target, out_weight):
    vmem = pl.BlockSpec(memory_space=pltpu.VMEM)
    smem = pl.BlockSpec(memory_space=pltpu.SMEM)
    anywhere = pl.BlockSpec(memory_space=pl.ANY)
    dma = pltpu.SemaphoreType.DMA
    out, moved = pl.pallas_call(
        kernel,
        out_shape=(
            jax.ShapeDtypeStruct((DRAFTS * REQ, COLS), BF16),
            jax.ShapeDtypeStruct((SLOTS, 2, ROWS, DIM), BF16),
        ),
        in_specs=[vmem, vmem, anywhere, smem, smem, vmem, vmem, vmem, anywhere],
        out_specs=(vmem, anywhere),
        scratch_shapes=[
            pltpu.VMEM((SLOTS + 1, 2, ROWS, DIM), BF16),
            pltpu.VMEM((HEADS * DIM, TPS * COLS), BF16),
            pltpu.VMEM((8, DIM), I32),
            pltpu.SMEM((8, DIM), I32),
            pltpu.VMEM((SLOTS, 2, ROWS, DIM), BF16),
            pltpu.VMEM((REQS, LINES, DIM), BF16),
            pltpu.VMEM((REQ, 2, 8, DIM), F32),
            pltpu.VMEM((REQ * LINES, DIM), F32),
            pltpu.VMEM((REQ, DIM), F32),
            pltpu.VMEM((REQ, DIM), F32),
            pltpu.VMEM((GROUPS, ROWS, DIM), F32),
            pltpu.VMEM((GROUPS, DIM), F32),
            pltpu.VMEM((GROUPS, DIM), F32),
            pltpu.VMEM((REQS, DIM), F32),
            pltpu.VMEM((REQS, DIM), F32),
            pltpu.VMEM((SLOTS * LINES, DIM), F32),
            pltpu.VMEM((2, CHIPS, TILES, 16, DIM), BF16),
            pltpu.VMEM((2, CHIPS, REQ, DIM), F32),
            pltpu.VMEM((CHIPS, TILES, 16, DIM), BF16),
            pltpu.VMEM((CHIPS, REQ, DIM), F32),
            pltpu.VMEM((CHIPS, TILES, 16, DIM), BF16),
            pltpu.VMEM((CHIPS, REQ, DIM), F32),
            pltpu.VMEM((CHIPS, TILES, 16, DIM), BF16),
            pltpu.VMEM((CHIPS, REQ, DIM), F32),
            pltpu.VMEM((CHIPS, REQ, DIM), F32),
            pltpu.VMEM((TILES, 16, DIM), F32),
            pltpu.VMEM((DRAFTS * REQ, HEADS * DIM), BF16),
            pltpu.VMEM((TPS, DRAFTS * REQ, COLS), BF16),
            pltpu.VMEM((TPS, DRAFTS * REQ, COLS), BF16),
            pltpu.VMEM((DRAFTS * REQ, COLS), F32),
            dma((3,)), dma,
            dma((CHIPS,)), dma((CHIPS,)), dma((CHIPS,)), dma((CHIPS,)),
            dma((INSTS,)), dma((INSTS,)), dma((2,)), dma((2,)),
            dma((CHIPS,)), dma((CHIPS,)), dma((CHIPS,)), dma((CHIPS,)),
            dma((TPS,)), dma((TPS,)),
        ],
        compiler_params=pltpu.CompilerParams(
            collective_id=0, has_side_effects=True, vmem_limit_bytes=48 << 20
        ),
        name="decode",
    )(
        queries.reshape(REQ, LINES, DIM),
        new_kv.reshape(REQ, 2, DRAFTS, DIM),
        kv_cache.reshape(SLOTS, 2, ROWS, DIM),
        block_owner,
        block_fill,
        move_slot.reshape(MOVES, 1),
        move_target,
        move_target.reshape(1, MOVES),
        out_weight,
    )
    return out, moved.reshape(kv_cache.shape)


def solution(mesh):
    placed = (
        P("inst", None, "tp", None),
        P("inst", None, None, "tp", None),
        P("inst", None, "tp", None, None),
        P("inst"),
        P("inst"),
        P("inst"),
        P("inst", None),
        P("tp", None),
    )
    return jax.shard_map(
        shards,
        mesh=mesh,
        in_specs=placed,
        out_specs=(P("inst", "tp"), P("inst", None, "tp", None, None)),
        check_vma=False,
    )
```

```python
import functools

import jax
import jax.numpy as jnp
from jax import lax
from jax.experimental import pallas as pl
from jax.experimental.pallas import tpu as pltpu
from jax.sharding import PartitionSpec as P

MESH = pl.DeviceIdType.MESH
MASKED = -1e30
CAPACITY = 2
F32, BF16, I32 = jnp.float32, jnp.bfloat16, jnp.int32

INSTS = 32
CHIPS = 16
TPS = 8
SLOTS = 64
ROWS = 64
DIM = 128
HEADS = 8
DRAFTS = 4
LINES = DRAFTS * HEADS
REQ = 8
REQS = INSTS * REQ
GROUPS = SLOTS // 4
TILES = LINES // 2
COLS = 512
MOVES = 24
EARLY = 12
WIDE = 2


def nt_dot(a, b):
    return lax.dot_general(a, b, (((1,), (1,)), ((), ())), preferred_element_type=F32)


def tile_lines(tile):
    t, g = 2 * (tile // HEADS), tile % HEADS
    return t * HEADS + g, (t + 1) * HEADS + g


def spread(weights, tile):
    first, second = tile_lines(tile)
    return jnp.concatenate(
        [
            jnp.broadcast_to(weights[:, first : first + 1], (REQ, DIM)),
            jnp.broadcast_to(weights[:, second : second + 1], (REQ, DIM)),
        ],
        axis=0,
    )


def kernel(
    q_hbm, nkv_hbm, kv_hbm, owner_hbm, fill_hbm, slot_hbm, target_hbm, w_hbm,
    out, moved,
    q, nkv, kv, w, owner, fill, slot, target, pick, pick_s, msend, qall, dkv, dval, dmax, dsum,
    score, smax, ssum, reqmax, reqsum, val, pay, aux, epay, eaux, cpay, caux,
    rpay, raux, spay, saux, fpay, faux, acc, att, zsend, zrecv, zout,
    load_sem, own_sem, ag_s, ag_r, sib_s, sib_r, mig_s, mig_r, e_s, e_r,
    p_s, p_r, a_s, a_r, fp_s, fp_r, fa_s, fa_r, z_s, z_r,
):
    me, tp = lax.axis_index("inst"), lax.axis_index("tp")
    core = lax.rem(me, 2)
    chip = me // 2
    sibling = me ^ 1

    def remote(src, dst, send, recv, inst, z):
        return pltpu.make_async_remote_copy(
            src_ref=src, dst_ref=dst, send_sem=send, recv_sem=recv,
            device_id=(inst, z), device_id_type=MESH,
        )

    barrier = pltpu.get_barrier_semaphore()

    @pl.loop(1, INSTS)
    def _(k):
        pl.semaphore_signal(barrier, inc=1, device_id=(me ^ k, tp), device_id_type=MESH)

    @pl.loop(1, TPS)
    def _(k):
        pl.semaphore_signal(barrier, inc=1, device_id=(me, tp ^ k), device_id_type=MESH)

    loads = [
        pltpu.make_async_copy(src, dst, load_sem.at[i])
        for i, (src, dst) in enumerate(
            [
                (q_hbm, q),
                (slot_hbm, slot),
                (target_hbm, target),
                (nkv_hbm, nkv),
                (owner_hbm, owner),
                (fill_hbm, fill),
                (kv_hbm, kv.at[pl.ds(0, SLOTS)]),
                (w_hbm, w),
                (pick, pick_s),
            ]
        )
    ]
    q_load, slot_load, target_load, nkv_load, owner_load, fill_load, kv_load, w_load, pick_load = loads
    for load in loads[:-1]:
        load.start()

    lane = lax.broadcasted_iota(I32, (1, DIM), 1)
    lane_group = lane // LINES

    def by_group(parts):
        return jnp.where(
            lane_group == 0,
            parts[0],
            jnp.where(lane_group == 1, parts[1], jnp.where(lane_group == 2, parts[2], parts[3])),
        )

    kv[SLOTS] = jnp.zeros((2, ROWS, DIM), BF16)
    dkv[...] = jnp.zeros(dkv.shape, F32)
    slot_load.wait()
    target_load.wait()
    pick_first = jnp.full((1, DIM), SLOTS, I32)
    pick_second = pick_first
    for j in range(MOVES):
        hit = lane == target[j]
        again = hit & (pick_first != SLOTS)
        pick_second = jnp.where(again, slot[j], pick_second)
        pick_first = jnp.where(hit & (pick_first == SLOTS), slot[j], pick_first)
    pick[...] = jnp.concatenate([pick_first, pick_second] * 4, axis=0)
    pick_load.start()

    def drafts():
        dkv[:, :, 0:DRAFTS, :] = nkv[...].astype(F32)
        for half in range(REQ // 4):
            queries = q[4 * half : 4 * half + 4].reshape(4 * LINES, DIM)
            keys = dkv[4 * half : 4 * half + 4, 0].reshape(4 * 8, DIM).astype(BF16)
            full = nt_dot(keys, queries)
            scores = by_group([full[8 * i : 8 * i + 8] for i in range(4)]) * (DIM**-0.5)
            u = lax.broadcasted_iota(I32, (8, DIM), 0)
            t = lax.rem(lax.broadcasted_iota(I32, (8, DIM), 1), LINES) // HEADS
            causal = u <= t
            high = jnp.max(jnp.where(causal, scores, MASKED), axis=0, keepdims=True)
            probs = jnp.where(causal, jnp.exp(scores - high), 0.0)
            total = jnp.sum(probs, axis=0, keepdims=True)
            turned = jnp.transpose(probs).astype(BF16)
            for i in range(4):
                r = 4 * half + i
                dmax[r : r + 1, :] = high if i == 0 else pltpu.roll(high, DIM - i * LINES, 1)
                dsum[r : r + 1, :] = total if i == 0 else pltpu.roll(total, DIM - i * LINES, 1)
                dval[r * LINES : (r + 1) * LINES, :] = jnp.dot(
                    turned[i * LINES : (i + 1) * LINES],
                    dkv[r, 1].astype(BF16),
                    preferred_element_type=F32,
                )

    q_load.wait()
    qall[pl.ds(me * 2, 2)] = q[...].reshape(2, REQ // 2, LINES, DIM)

    def chunk(kx, ky, h):
        return qall.at[(me ^ (kx * 8 + ky * 2)) * 2 + h]

    def gather(kx, ky, h):
        first, on = ((kx * 8, ky * 2), (ky * 2, kx * 8))[h]
        if on == 0:
            src, to = chunk(0, 0, h), me ^ first
        else:
            src, to = (chunk(kx, 0, h), chunk(0, ky, h))[h], me ^ on
        at = h * CHIPS + kx * 4 + ky
        return remote(src, src, ag_s.at[at], ag_r.at[at], to, tp)

    def arrived(kx, ky, h):
        at = h * CHIPS + kx * 4 + ky
        ref = chunk(kx, ky, h)
        return remote(ref, ref, ag_s.at[at], ag_r.at[at], sibling, tp)

    def gather_on(kx, ky, h):
        at = h * CHIPS + kx * 4 + ky
        ref = chunk(kx, ky, h)
        return remote(ref, ref, sib_s.at[at], sib_r.at[at], sibling, tp)

    order = (1, 3, 2)
    pl.semaphore_wait(barrier, INSTS - 1 + TPS - 1)
    for k in (2, 1, 3):
        gather(k, 0, 0).start()
        gather(0, k, 1).start()
    for k in (2, 1, 3):
        gather(0, k, 0).start()
        gather(k, 0, 1).start()
    gather_on(0, 0, 0).start()
    gather_on(0, 0, 1).start()
    nkv_load.wait()
    drafts()
    for a in order:
        arrived(a, 0, 0).wait_recv()
        for b in (2, 1, 3):
            gather(a, b, 0).start()
        arrived(0, a, 1).wait_recv()
        for b in (2, 1, 3):
            gather(b, a, 1).start()
        gather_on(a, 0, 0).start()
        gather_on(0, a, 1).start()

    kv_load.wait()
    pick_load.wait()

    @pl.loop(0, INSTS)
    def _(d):
        for i in range(CAPACITY):
            msend[CAPACITY * d + i] = kv[pick_s[i, d]]

    for a in (0,) + order:
        for b in order:
            arrived(a, b, 0).wait_recv()
            gather_on(a, b, 0).start()
            arrived(b, a, 1).wait_recv()
            gather_on(b, a, 1).start()

    own = pltpu.make_async_copy(
        msend.at[pl.ds(CAPACITY * me, CAPACITY)],
        moved.at[pl.ds(CAPACITY * me, CAPACITY)],
        own_sem,
    )
    own.start()

    def migrate(i):
        k = lax.rem(i * 11, INSTS)
        return remote(
            msend.at[pl.ds(CAPACITY * (me ^ k), CAPACITY)],
            moved.at[pl.ds(CAPACITY * me, CAPACITY)],
            mig_s.at[k], mig_r.at[k], me ^ k, tp,
        )

    @pl.loop(1, 1 + EARLY)
    def _(i):
        migrate(i).start()

    owner_load.wait()
    fill_load.wait()
    for a in range(4):
        for b in range(4):
            for h in range(2):
                gather_on(a, b, h).wait_recv()

    row_of = lax.broadcasted_iota(I32, (ROWS, DIM), 0)

    def usable(g):
        return row_of < by_group([fill[4 * g + i] for i in range(4)])

    def score_group(g):
        queries = jnp.concatenate(
            [qall[owner[4 * g + i] // 4, lax.rem(owner[4 * g + i], 4)] for i in range(4)], axis=0
        )
        keys = kv[pl.ds(4 * g, 4), 0].reshape(4 * ROWS, DIM)
        full = nt_dot(keys, queries)
        scores = by_group([full[ROWS * i : ROWS * (i + 1)] for i in range(4)]) * (DIM**-0.5)
        scores = jnp.where(usable(g), scores, MASKED)
        return scores, jnp.max(scores, axis=0, keepdims=True)

    row = lax.broadcasted_iota(I32, (REQS, DIM), 0)
    request = (row % (REQS // 2)) // REQ * (2 * REQ) + row // (REQS // 2) * REQ + row % REQ

    def owners(g):
        return by_group([owner[4 * g + i] for i in range(4)])

    def all_groups(x, f):
        x = f(x, pltpu.roll(x, 2 * LINES, 1))
        return f(x, pltpu.roll(x, LINES, 1))

    def weigh_group(g, scores):
        highs = []
        for i in range(4):
            o = owner[4 * g + i]
            at = lax.rem(o // REQ, 2) * (REQS // 2) + o // (2 * REQ) * REQ + lax.rem(o, REQ)
            highs.append(reqmax[pl.ds(at, 1), :])
        probs = jnp.where(usable(g), jnp.exp(scores - by_group(highs)), 0.0)
        turned = jnp.transpose(probs).astype(BF16)
        return jnp.sum(probs, axis=0, keepdims=True), [
            jnp.dot(
                turned[i * LINES : (i + 1) * LINES],
                kv[4 * g + i, 1],
                preferred_element_type=F32,
            )
            for i in range(4)
        ]

    @pl.loop(0, GROUPS // WIDE)
    def _(s):
        for g in [s * WIDE + i for i in range(WIDE)]:
            score[g], smax[pl.ds(g, 1), :] = score_group(g)

    reqmax[...] = jnp.full(reqmax.shape, MASKED, F32)

    @pl.loop(0, GROUPS // 4)
    def _(s):
        high = reqmax[...]
        for g in [s * 4 + i for i in range(4)]:
            high = jnp.where(
                request == owners(g), jnp.maximum(high, smax[pl.ds(g, 1), :]), high
            )
        reqmax[...] = high

    reqmax[...] = all_groups(reqmax[...], jnp.maximum)

    @pl.loop(0, GROUPS // WIDE)
    def _(s):
        groups = [s * WIDE + i for i in range(WIDE)]
        done = [weigh_group(g, score[g]) for g in groups]
        for g, (total, values) in zip(groups, done):
            ssum[pl.ds(g, 1), :] = total
            for i in range(4):
                val[pl.ds((4 * g + i) * LINES, LINES), :] = values[i]

    reqsum[...] = jnp.zeros(reqsum.shape, F32)

    @pl.loop(0, GROUPS // 4)
    def _(s):
        total = reqsum[...]
        for g in [s * 4 + i for i in range(4)]:
            total += jnp.where(request == owners(g), ssum[pl.ds(g, 1), :], 0.0)
        reqsum[...] = total

    reqsum[...] = all_groups(reqsum[...], jnp.add)
    aux[...] = jnp.where(lane < LINES, reqmax[...], reqsum[...]).reshape(aux.shape)

    owner_lane = lax.broadcasted_iota(I32, (1, SLOTS), 1)

    def owner_step(b, x):
        return jnp.where(owner_lane == b, owner[b], x)

    half_row = lax.broadcasted_iota(I32, (REQS // 2, SLOTS), 0)

    def sum_slots(home_core, half, owner_row):
        ids = half_row // REQ * (2 * REQ) + home_core * REQ + half_row % REQ
        member = (ids == owner_row).astype(F32).astype(BF16)

        @pl.loop(0, HEADS // 2)
        def _(s):
            done = []
            for g in [s * 2 + i for i in range(2)]:
                first = 2 * HEADS * half + g
                lines = jnp.concatenate(
                    [
                        val[pl.ds(first, SLOTS, stride=LINES), :],
                        val[pl.ds(first + HEADS, SLOTS, stride=LINES), :],
                    ],
                    axis=1,
                ).astype(BF16)
                done.append((g, jnp.dot(member, lines, preferred_element_type=F32)))
            for g, summed in done:
                for c in range(CHIPS):
                    both = summed[c * REQ : (c + 1) * REQ]
                    pay[home_core, half, c, g] = jnp.concatenate(
                        [both[:, :DIM], both[:, DIM:]], axis=0
                    ).astype(BF16)

    def join_cores(half):
        return remote(pay.at[1 - core, half], epay.at[half], e_s.at[half], e_r.at[half], sibling, tp)

    aux_join = remote(aux.at[1 - core], eaux, e_s.at[2], e_r.at[2], sibling, tp)

    def join(half, k, into, aux_into):
        @pl.loop(0, 4)
        def _(m):
            home = chip ^ (k * 4 + m if half == 0 else m * 4 + k)
            a, b = aux[core, home], eaux[home]
            high = jnp.maximum(a, b)
            wa, wb = jnp.exp(a - high), jnp.exp(b - high)
            total = pltpu.roll(wa, LINES, 1) * a + pltpu.roll(wb, LINES, 1) * b
            aux_into[half, k, m] = jnp.where(lane < LINES, high, total)
            for g in range(HEADS):
                tile = half * HEADS + g
                into[half, k, m, g] = (
                    spread(wa, tile) * pay[core, half, home, g].astype(F32)
                    + spread(wb, tile) * epay[half, home, g].astype(F32)
                ).astype(BF16)

    def step_of(half, k):
        return me ^ (k * 8 if half == 0 else k * 2)

    def first_pay(half, k):
        at = half * 4 + k
        return remote(
            cpay.at[half, k], rpay.at[half, k], p_s.at[at], p_r.at[at], step_of(half, k), tp
        )

    def first_aux(half, k):
        at = half * 4 + k
        return remote(
            caux.at[half, k], raux.at[half, k], a_s.at[at], a_r.at[at], step_of(half, k), tp
        )

    def second_pay(half, m):
        at = half * 4 + m
        return remote(
            spay.at[half, m], fpay.at[half, m], fp_s.at[at], fp_r.at[at], step_of(1 - half, m), tp
        )

    def second_aux(half, m):
        at = half * 4 + m
        return remote(
            saux.at[half, m], faux.at[half, m], fa_s.at[at], fa_r.at[at], step_of(1 - half, m), tp
        )

    def merge(half, m, into, aux_into):
        parts = [raux[half, k, m] for k in range(4)]
        high = functools.reduce(jnp.maximum, parts)
        weights = [jnp.exp(part - high) for part in parts]
        total = sum(pltpu.roll(wt, LINES, 1) * part for wt, part in zip(weights, parts))
        aux_into[half, m] = jnp.where(lane < LINES, high, total)
        for g in range(HEADS):
            tile = half * HEADS + g
            into[half, m, g] = sum(
                spread(weights[k], tile) * rpay[half, k, m, g].astype(F32) for k in range(4)
            ).astype(BF16)

    aux_join.start()
    owner_row = lax.fori_loop(0, SLOTS, owner_step, jnp.zeros((1, SLOTS), I32))
    for half in range(2):
        sum_slots(1 - core, half, owner_row)
        join_cores(half).start()
    for half in range(2):
        sum_slots(core, half, owner_row)
    aux_join.wait()
    join_cores(0).wait()
    join_cores(1).wait()

    for k in (2, 1, 3):
        for half in range(2):
            join(half, k, cpay, caux)
            first_aux(half, k).start()
            first_pay(half, k).start()
    for half in range(2):
        join(half, 0, rpay, raux)
    for k in (1, 3, 2):
        for half in range(2):
            first_aux(half, k).wait_recv()
            first_pay(half, k).wait_recv()
    for m in (2, 1, 3):
        for half in range(2):
            merge(half, m, spay, saux)
            second_aux(half, m).start()
            second_pay(half, m).start()
    for half in range(2):
        merge(half, 0, fpay, faux)
    for half in range(2):
        for m in (1, 3, 2):
            second_aux(half, m).wait_recv()

    parts = [
        jnp.where(lane % LINES < LINES // 2, faux[0, m], faux[1, m]) for m in range(4)
    ]
    peak = functools.reduce(jnp.maximum, parts, dmax[...])
    weights = [jnp.exp(part - peak) for part in parts]
    draft_weight = jnp.exp(dmax[...] - peak)
    total = draft_weight * dsum[...] + sum(
        wt * pltpu.roll(part, DIM - LINES, 1) for wt, part in zip(weights, parts)
    )
    scale = 1.0 / total
    weights = [wt * scale for wt in weights]
    draft_weight = draft_weight * scale
    for tile in range(TILES):
        first, second = tile_lines(tile)
        acc[tile] = spread(draft_weight, tile) * jnp.concatenate(
            [
                dval[pl.ds(first, REQ, stride=LINES), :],
                dval[pl.ds(second, REQ, stride=LINES), :],
            ],
            axis=0,
        )
    for half in range(2):
        for m in (1, 3, 2):
            second_pay(half, m).wait_recv()
    for tile in range(TILES):
        half, g = tile // HEADS, tile % HEADS
        line = acc[tile] + sum(
            spread(weights[m], tile) * fpay[half, m, g].astype(F32) for m in range(4)
        )
        att[half * 16 : (half + 1) * 16, g * DIM : (g + 1) * DIM] = line.astype(BF16)

    @pl.loop(1 + EARLY, INSTS)
    def _(i):
        migrate(i).start()

    w_load.wait()

    def project(k):
        columns = pl.ds(pl.multiple_of(lax.rem(tp + k, TPS) * COLS, COLS), COLS)
        return jnp.dot(att[...], w[:, columns], preferred_element_type=F32)

    def send_columns(k):
        return remote(
            zsend.at[k], zrecv.at[k], z_s.at[k], z_r.at[k], me, lax.rem(tp + k, TPS)
        )

    for k in (4, 3, 5, 2, 6, 1, 7):
        zsend[k] = project(k).astype(BF16)
        send_columns(k).start()

    zout[...] = project(0)

    for k in (1, 7, 2, 6, 3, 5, 4):
        send_columns(k).wait_recv()
        zout[...] += zrecv[k].astype(F32)

    for t in range(DRAFTS):
        for c in range(COLS // DIM):
            dval[pl.ds(c * 32 + t, REQ, stride=DRAFTS), :] = zout[
                t * REQ : (t + 1) * REQ, c * DIM : (c + 1) * DIM
            ]
    for c in range(COLS // DIM):
        out[:, c * DIM : (c + 1) * DIM] = dval[c * 32 : (c + 1) * 32, :].astype(BF16)

    for a in range(4):
        for b in range(4):
            for h in range(2):
                if (a, b) != (0, 0):
                    gather(a, b, h).wait_send()
                gather_on(a, b, h).wait_send()
    own.wait()
    for half in range(2):
        for k in range(1, 4):
            first_aux(half, k).wait_send()
            first_pay(half, k).wait_send()
            second_aux(half, k).wait_send()
            second_pay(half, k).wait_send()
    for k in range(1, TPS):
        send_columns(k).wait_send()
    @pl.loop(1, INSTS)
    def _(i):
        migrate(i).wait()


def shards(queries, new_kv, kv_cache, block_owner, block_fill, move_slot, move_target, out_weight):
    vmem = pl.BlockSpec(memory_space=pltpu.VMEM)
    anywhere = pl.BlockSpec(memory_space=pl.ANY)
    dma = pltpu.SemaphoreType.DMA
    out, moved = pl.pallas_call(
        kernel,
        out_shape=(
            jax.ShapeDtypeStruct((DRAFTS * REQ, COLS), BF16),
            jax.ShapeDtypeStruct((SLOTS, 2, ROWS, DIM), BF16),
        ),
        in_specs=[anywhere] * 8,
        out_specs=(vmem, anywhere),
        scratch_shapes=[
            pltpu.VMEM((REQ, LINES, DIM), BF16),
            pltpu.VMEM((REQ, 2, DRAFTS, DIM), BF16),
            pltpu.VMEM((SLOTS + 1, 2, ROWS, DIM), BF16),
            pltpu.VMEM((HEADS * DIM, TPS * COLS), BF16),
            pltpu.SMEM((SLOTS,), I32),
            pltpu.SMEM((SLOTS,), I32),
            pltpu.SMEM((MOVES,), I32),
            pltpu.SMEM((MOVES,), I32),
            pltpu.VMEM((8, DIM), I32),
            pltpu.SMEM((8, DIM), I32),
            pltpu.VMEM((SLOTS, 2, ROWS, DIM), BF16),
            pltpu.VMEM((INSTS * 2, REQ // 2, LINES, DIM), BF16),
            pltpu.VMEM((REQ, 2, 8, DIM), F32),
            pltpu.VMEM((REQ * LINES, DIM), F32),
            pltpu.VMEM((REQ, DIM), F32),
            pltpu.VMEM((REQ, DIM), F32),
            pltpu.VMEM((GROUPS, ROWS, DIM), F32),
            pltpu.VMEM((GROUPS, DIM), F32),
            pltpu.VMEM((GROUPS, DIM), F32),
            pltpu.VMEM((REQS, DIM), F32),
            pltpu.VMEM((REQS, DIM), F32),
            pltpu.VMEM((SLOTS * LINES, DIM), F32),
            pltpu.VMEM((2, 2, CHIPS, HEADS, 16, DIM), BF16),
            pltpu.VMEM((2, CHIPS, REQ, DIM), F32),
            pltpu.VMEM((2, CHIPS, HEADS, 16, DIM), BF16),
            pltpu.VMEM((CHIPS, REQ, DIM), F32),
            pltpu.VMEM((2, 4, 4, HEADS, 16, DIM), BF16),
            pltpu.VMEM((2, 4, 4, REQ, DIM), F32),
            pltpu.VMEM((2, 4, 4, HEADS, 16, DIM), BF16),
            pltpu.VMEM((2, 4, 4, REQ, DIM), F32),
            pltpu.VMEM((2, 4, HEADS, 16, DIM), BF16),
            pltpu.VMEM((2, 4, REQ, DIM), F32),
            pltpu.VMEM((2, 4, HEADS, 16, DIM), BF16),
            pltpu.VMEM((2, 4, REQ, DIM), F32),
            pltpu.VMEM((TILES, 16, DIM), F32),
            pltpu.VMEM((DRAFTS * REQ, HEADS * DIM), BF16),
            pltpu.VMEM((TPS, DRAFTS * REQ, COLS), BF16),
            pltpu.VMEM((TPS, DRAFTS * REQ, COLS), BF16),
            pltpu.VMEM((DRAFTS * REQ, COLS), F32),
            dma((9,)), dma,
            dma((2 * CHIPS,)), dma((2 * CHIPS,)), dma((2 * CHIPS,)), dma((2 * CHIPS,)),
            dma((INSTS,)), dma((INSTS,)), dma((3,)), dma((3,)),
            dma((8,)), dma((8,)), dma((8,)), dma((8,)),
            dma((8,)), dma((8,)), dma((8,)), dma((8,)),
            dma((TPS,)), dma((TPS,)),
        ],
        compiler_params=pltpu.CompilerParams(
            collective_id=0, has_side_effects=True, vmem_limit_bytes=63 << 20
        ),
        name="decode",
    )(
        queries.reshape(REQ, LINES, DIM),
        new_kv.reshape(REQ, 2, DRAFTS, DIM),
        kv_cache.reshape(SLOTS, 2, ROWS, DIM),
        block_owner,
        block_fill,
        move_slot,
        move_target.reshape(MOVES),
        out_weight,
    )
    return out, moved.reshape(kv_cache.shape)


def solution(mesh):
    placed = (
        P("inst", None, "tp", None),
        P("inst", None, None, "tp", None),
        P("inst", None, "tp", None, None),
        P("inst"),
        P("inst"),
        P("inst"),
        P("inst", None),
        P("tp", None),
    )
    return jax.shard_map(
        shards,
        mesh=mesh,
        in_specs=placed,
        out_specs=(P("inst", "tp"), P("inst", None, "tp", None, None)),
        check_vma=False,
    )
```

```python
import functools

import jax
import jax.numpy as jnp
from jax import lax
from jax.experimental import pallas as pl
from jax.experimental.pallas import tpu as pltpu
from jax.sharding import PartitionSpec as P

MESH = pl.DeviceIdType.MESH
MASKED = -1e30
CAPACITY = 2
F32, BF16, I32 = jnp.float32, jnp.bfloat16, jnp.int32

INSTS = 32
CHIPS = 16
TPS = 8
SLOTS = 64
ROWS = 64
DIM = 128
HEADS = 8
DRAFTS = 4
LINES = DRAFTS * HEADS
REQ = 8
REQS = INSTS * REQ
GROUPS = SLOTS // 4
TILES = LINES // 2
COLS = 512
MOVES = 24
BATCHES = (8, 10, 2, 0, 4)
WIDE = 4
PARTS = 8
SUMS = 4


def nt_dot(a, b):
    return lax.dot_general(a, b, (((1,), (1,)), ((), ())), preferred_element_type=F32)


def tile_lines(tile):
    t, g = 2 * (tile // HEADS), tile % HEADS
    return t * HEADS + g, (t + 1) * HEADS + g


def spread(weights, tile):
    first, second = tile_lines(tile)
    return jnp.concatenate(
        [
            jnp.broadcast_to(weights[:, first : first + 1], (REQ, DIM)),
            jnp.broadcast_to(weights[:, second : second + 1], (REQ, DIM)),
        ],
        axis=0,
    )


def kernel(
    q_hbm, nkv_hbm, kv_hbm, owner_hbm, fill_hbm, slot_hbm, target_hbm, w_hbm,
    out, moved,
    q, nkv, kv, w, owner, fill, slot, target, pick, pick_s, msend, qall, dkv, dval, dmax, dsum,
    score, smax, ssum, reqmax, reqsum, val, pay, aux, epay, eaux, cpay,
    rpay, spay, fpay, acc, att, zsend, zrecv, zout,
    load_sem, own_sem, ag_s, ag_r, sib_s, sib_r, mig_s, mig_r, e_s, e_r,
    p_s, p_r, fp_s, fp_r, z_s, z_r,
):
    me, tp = lax.axis_index("inst"), lax.axis_index("tp")
    core = lax.rem(me, 2)
    chip = me // 2
    sibling = me ^ 1

    def remote(src, dst, send, recv, inst, z):
        return pltpu.make_async_remote_copy(
            src_ref=src, dst_ref=dst, send_sem=send, recv_sem=recv,
            device_id=(inst, z), device_id_type=MESH,
        )

    barrier = pltpu.get_barrier_semaphore()

    @pl.loop(1, INSTS)
    def _(k):
        pl.semaphore_signal(barrier, inc=1, device_id=(me ^ k, tp), device_id_type=MESH)

    @pl.loop(1, TPS)
    def _(k):
        pl.semaphore_signal(barrier, inc=1, device_id=(me, tp ^ k), device_id_type=MESH)

    loads = [
        pltpu.make_async_copy(src, dst, load_sem.at[i])
        for i, (src, dst) in enumerate(
            [
                (q_hbm, q),
                (slot_hbm, slot),
                (target_hbm, target),
                (nkv_hbm, nkv),
                (owner_hbm, owner),
                (fill_hbm, fill),
                (kv_hbm, kv.at[pl.ds(0, SLOTS)]),
                (w_hbm, w),
                (pick, pick_s),
            ]
        )
    ]
    q_load, slot_load, target_load, nkv_load, owner_load, fill_load, kv_load, w_load, pick_load = loads
    for load in loads[:-1]:
        load.start()

    lane = lax.broadcasted_iota(I32, (1, DIM), 1)
    lane_group = lane // LINES

    def by_group(parts):
        return jnp.where(
            lane_group == 0,
            parts[0],
            jnp.where(lane_group == 1, parts[1], jnp.where(lane_group == 2, parts[2], parts[3])),
        )

    kv[SLOTS] = jnp.zeros((2, ROWS, DIM), BF16)
    dkv[...] = jnp.zeros(dkv.shape, F32)
    slot_load.wait()
    target_load.wait()
    pick_first = jnp.full((1, DIM), SLOTS, I32)
    pick_second = pick_first
    for j in range(MOVES):
        hit = lane == target[j]
        again = hit & (pick_first != SLOTS)
        pick_second = jnp.where(again, slot[j], pick_second)
        pick_first = jnp.where(hit & (pick_first == SLOTS), slot[j], pick_first)
    pick[...] = jnp.concatenate([pick_first, pick_second] * 4, axis=0)
    pick_load.start()

    def drafts():
        dkv[:, :, 0:DRAFTS, :] = nkv[...].astype(F32)
        for half in range(REQ // 4):
            queries = q[4 * half : 4 * half + 4].reshape(4 * LINES, DIM)
            keys = dkv[4 * half : 4 * half + 4, 0].reshape(4 * 8, DIM).astype(BF16)
            full = nt_dot(keys, queries)
            scores = by_group([full[8 * i : 8 * i + 8] for i in range(4)]) * (DIM**-0.5)
            u = lax.broadcasted_iota(I32, (8, DIM), 0)
            t = lax.rem(lax.broadcasted_iota(I32, (8, DIM), 1), LINES) // HEADS
            causal = u <= t
            high = jnp.max(jnp.where(causal, scores, MASKED), axis=0, keepdims=True)
            probs = jnp.where(causal, jnp.exp(scores - high), 0.0)
            total = jnp.sum(probs, axis=0, keepdims=True)
            turned = jnp.transpose(probs).astype(BF16)
            for i in range(4):
                r = 4 * half + i
                dmax[r : r + 1, :] = high if i == 0 else pltpu.roll(high, DIM - i * LINES, 1)
                dsum[r : r + 1, :] = total if i == 0 else pltpu.roll(total, DIM - i * LINES, 1)
                dval[r * LINES : (r + 1) * LINES, :] = jnp.dot(
                    turned[i * LINES : (i + 1) * LINES],
                    dkv[r, 1].astype(BF16),
                    preferred_element_type=F32,
                )

    q_load.wait()
    qall[pl.ds(me * 2, 2)] = q[...].reshape(2, REQ // 2, LINES, DIM)

    def chunk(kx, ky, h):
        return qall.at[(me ^ (kx * 8 + ky * 2)) * 2 + h]

    def gather(kx, ky, h):
        first, on = ((kx * 8, ky * 2), (ky * 2, kx * 8))[h]
        if on == 0:
            src, to = chunk(0, 0, h), me ^ first
        else:
            src, to = (chunk(kx, 0, h), chunk(0, ky, h))[h], me ^ on
        at = h * CHIPS + kx * 4 + ky
        return remote(src, src, ag_s.at[at], ag_r.at[at], to, tp)

    def arrived(kx, ky, h):
        at = h * CHIPS + kx * 4 + ky
        ref = chunk(kx, ky, h)
        return remote(ref, ref, ag_s.at[at], ag_r.at[at], sibling, tp)

    def gather_on(kx, ky, h):
        at = h * CHIPS + kx * 4 + ky
        ref = chunk(kx, ky, h)
        return remote(ref, ref, sib_s.at[at], sib_r.at[at], sibling, tp)

    def migrate(i):
        k = lax.rem(i * 11, INSTS)
        return remote(
            msend.at[pl.ds(CAPACITY * (me ^ k), CAPACITY)],
            moved.at[pl.ds(CAPACITY * me, CAPACITY)],
            mig_s.at[k], mig_r.at[k], me ^ k, tp,
        )

    bounds = [1 + sum(BATCHES[:i]) for i in range(len(BATCHES) + 1)] + [INSTS]

    def migrate_batch(i):
        pl.loop(bounds[i], bounds[i + 1])(lambda k: migrate(k).start())

    order = (1, 3, 2)
    nkv_load.wait()
    drafts()

    kv_load.wait()
    pick_load.wait()

    @pl.loop(0, INSTS)
    def _(d):
        for i in range(CAPACITY):
            msend[CAPACITY * d + i] = kv[pick_s[i, d]]

    pl.semaphore_wait(barrier, INSTS - 1 + TPS - 1)
    for k in (2, 1, 3):
        gather(k, 0, 0).start()
        gather(0, k, 1).start()
    for k in (2, 1, 3):
        gather(0, k, 0).start()
        gather(k, 0, 1).start()
    gather_on(0, 0, 0).start()
    gather_on(0, 0, 1).start()
    for a in order:
        arrived(a, 0, 0).wait_recv()
        for b in (2, 1, 3):
            gather(a, b, 0).start()
        arrived(0, a, 1).wait_recv()
        for b in (2, 1, 3):
            gather(b, a, 1).start()
        gather_on(a, 0, 0).start()
        gather_on(0, a, 1).start()

    migrate_batch(0)

    for a in (0,) + order:
        for b in order:
            arrived(a, b, 0).wait_recv()
            gather_on(a, b, 0).start()
            arrived(b, a, 1).wait_recv()
            gather_on(b, a, 1).start()

    own = pltpu.make_async_copy(
        msend.at[pl.ds(CAPACITY * me, CAPACITY)],
        moved.at[pl.ds(CAPACITY * me, CAPACITY)],
        own_sem,
    )
    own.start()

    migrate_batch(1)
    owner_load.wait()
    fill_load.wait()
    for a in range(4):
        for b in range(4):
            for h in range(2):
                gather_on(a, b, h).wait_recv()

    row_of = lax.broadcasted_iota(I32, (ROWS, DIM), 0)

    def usable(g):
        return row_of < by_group([fill[4 * g + i] for i in range(4)])

    def score_group(g):
        queries = jnp.concatenate(
            [qall[owner[4 * g + i] // 4, lax.rem(owner[4 * g + i], 4)] for i in range(4)], axis=0
        )
        keys = kv[pl.ds(4 * g, 4), 0].reshape(4 * ROWS, DIM)
        full = nt_dot(keys, queries)
        scores = by_group([full[ROWS * i : ROWS * (i + 1)] for i in range(4)]) * (DIM**-0.5)
        scores = jnp.where(usable(g), scores, MASKED)
        return scores, jnp.max(scores, axis=0, keepdims=True)

    row = lax.broadcasted_iota(I32, (REQS, DIM), 0)
    request = (row % (REQS // 2)) // REQ * (2 * REQ) + row // (REQS // 2) * REQ + row % REQ

    def owners(g):
        return by_group([owner[4 * g + i] for i in range(4)])

    def all_groups(x, f):
        x = f(x, pltpu.roll(x, 2 * LINES, 1))
        return f(x, pltpu.roll(x, LINES, 1))

    def weigh_group(g, scores):
        highs = []
        for i in range(4):
            o = owner[4 * g + i]
            at = lax.rem(o // REQ, 2) * (REQS // 2) + o // (2 * REQ) * REQ + lax.rem(o, REQ)
            highs.append(reqmax[pl.ds(at, 1), :])
        probs = jnp.where(usable(g), jnp.exp(scores - by_group(highs)), 0.0)
        turned = jnp.transpose(probs).astype(BF16)
        return jnp.sum(probs, axis=0, keepdims=True), [
            jnp.dot(
                turned[i * LINES : (i + 1) * LINES],
                kv[4 * g + i, 1],
                preferred_element_type=F32,
            )
            for i in range(4)
        ]

    @pl.loop(0, GROUPS // WIDE)
    def _(s):
        for g in [s * WIDE + i for i in range(WIDE)]:
            score[g], smax[pl.ds(g, 1), :] = score_group(g)

    reqmax[...] = jnp.full(reqmax.shape, MASKED, F32)

    @pl.loop(0, GROUPS // 4)
    def _(s):
        high = reqmax[...]
        for g in [s * 4 + i for i in range(4)]:
            high = jnp.where(
                request == owners(g), jnp.maximum(high, smax[pl.ds(g, 1), :]), high
            )
        reqmax[...] = high

    reqmax[...] = all_groups(reqmax[...], jnp.maximum)

    @pl.loop(0, GROUPS // WIDE)
    def _(s):
        groups = [s * WIDE + i for i in range(WIDE)]
        done = [weigh_group(g, score[g]) for g in groups]
        for g, (total, values) in zip(groups, done):
            ssum[pl.ds(g, 1), :] = total
            for i in range(4):
                val[pl.ds((4 * g + i) * LINES, LINES), :] = values[i]

    owner_lane = lax.broadcasted_iota(I32, (1, SLOTS), 1)

    def owner_step(b, x):
        return jnp.where(owner_lane == b, owner[b], x)

    half_row = lax.broadcasted_iota(I32, (REQS // 2, SLOTS), 0)

    def sum_slots(home_core, half, owner_row):
        ids = half_row // REQ * (2 * REQ) + home_core * REQ + half_row % REQ
        member = (ids == owner_row).astype(F32).astype(BF16)

        @pl.loop(0, HEADS // SUMS)
        def _(s):
            done = []
            for g in [s * SUMS + i for i in range(SUMS)]:
                first = 2 * HEADS * half + g
                lines = jnp.concatenate(
                    [
                        val[pl.ds(first, SLOTS, stride=LINES), :],
                        val[pl.ds(first + HEADS, SLOTS, stride=LINES), :],
                    ],
                    axis=1,
                ).astype(BF16)
                done.append((g, jnp.dot(member, lines, preferred_element_type=F32)))
            for g, summed in done:
                for c in range(CHIPS):
                    both = summed[c * REQ : (c + 1) * REQ]
                    pay[home_core, half, c, g] = jnp.concatenate(
                        [both[:, :DIM], both[:, DIM:]], axis=0
                    ).astype(BF16)

    def join_cores(half):
        return remote(pay.at[1 - core, half], epay.at[half], e_s.at[half], e_r.at[half], sibling, tp)

    aux_join = remote(aux.at[1 - core], eaux, e_s.at[2], e_r.at[2], sibling, tp)

    def to_parts(x):
        high = x.astype(BF16).astype(F32)
        rest = x - high
        mid = rest.astype(BF16).astype(F32)
        top = jnp.where(lane < 2 * LINES, high, pltpu.roll(mid, 2 * LINES, 1))
        return jnp.concatenate([top, rest - mid], axis=0).astype(BF16)

    def from_parts(tile):
        tile = tile.astype(F32)
        top, low = tile[:REQ], tile[REQ:]
        return (top + pltpu.roll(top, 2 * LINES, 1)) + low

    def join(half, k, m, into):
        home = chip ^ (k * 4 + m if half == 0 else m * 4 + k)
        a, b = aux[core, home], eaux[home]
        high = jnp.maximum(a, b)
        wa, wb = jnp.exp(a - high), jnp.exp(b - high)
        total = pltpu.roll(wa, LINES, 1) * a + pltpu.roll(wb, LINES, 1) * b
        into[half, m, k, HEADS] = to_parts(jnp.where(lane < LINES, high, total))
        for g in range(HEADS):
            tile = half * HEADS + g
            into[half, m, k, g] = (
                spread(wa, tile) * pay[core, half, home, g].astype(F32)
                + spread(wb, tile) * epay[half, home, g].astype(F32)
            ).astype(BF16)

    def step_of(half, k):
        return me ^ (k * 8 if half == 0 else k * 2)

    def first_pay(half, m, k):
        at = (half * 4 + m) * 4 + k
        return remote(
            cpay.at[half, m, k], rpay.at[half, m, k], p_s.at[at], p_r.at[at], step_of(half, k), tp
        )

    def second_pay(half, m):
        at = half * 4 + m
        return remote(
            spay.at[half, m], fpay.at[half, m], fp_s.at[at], fp_r.at[at], step_of(1 - half, m), tp
        )

    def merge(half, m, into):
        parts = [from_parts(rpay[half, m, k, HEADS]) for k in range(4)]
        high = functools.reduce(jnp.maximum, parts)
        weights = [jnp.exp(part - high) for part in parts]
        total = sum(pltpu.roll(wt, LINES, 1) * part for wt, part in zip(weights, parts))
        into[half, m, HEADS] = to_parts(jnp.where(lane < LINES, high, total))
        for g in range(HEADS):
            tile = half * HEADS + g
            into[half, m, g] = sum(
                spread(weights[k], tile) * rpay[half, m, k, g].astype(F32) for k in range(4)
            ).astype(BF16)

    owner_row = lax.fori_loop(0, SLOTS, owner_step, jnp.zeros((1, SLOTS), I32))
    for half in range(2):
        sum_slots(1 - core, half, owner_row)
        join_cores(half).start()
    migrate_batch(2)

    reqsum[...] = jnp.zeros(reqsum.shape, F32)

    @pl.loop(0, GROUPS // 4)
    def _(s):
        total = reqsum[...]
        for g in [s * 4 + i for i in range(4)]:
            total += jnp.where(request == owners(g), ssum[pl.ds(g, 1), :], 0.0)
        reqsum[...] = total

    reqsum[...] = all_groups(reqsum[...], jnp.add)
    aux[...] = jnp.where(lane < LINES, reqmax[...], reqsum[...]).reshape(aux.shape)
    aux_join.start()
    for half in range(2):
        sum_slots(core, half, owner_row)
    aux_join.wait()
    join_cores(0).wait()

    for m in (2, 1, 3, 0):
        for half in range(2):
            if m == 2 and half == 1:
                join_cores(1).wait()

            @pl.loop(1, 4)
            def _(k):
                join(half, k, m, cpay)
                first_pay(half, m, k).start()

        if m == 1:
            migrate_batch(3)

    for half in range(2):
        pl.loop(0, 4)(lambda m: join(half, 0, m, rpay))

    for m in (2, 1, 3, 0):
        for half in range(2):
            for k in (1, 3, 2):
                first_pay(half, m, k).wait_recv()
            merge(half, m, fpay if m == 0 else spay)
            if m != 0:
                second_pay(half, m).start()
    migrate_batch(4)

    for half in range(2):
        for m in (1, 3, 2):
            second_pay(half, m).wait_recv()

    parts = [
        jnp.where(
            lane % LINES < LINES // 2,
            from_parts(fpay[0, m, HEADS]),
            from_parts(fpay[1, m, HEADS]),
        )
        for m in range(4)
    ]
    peak = functools.reduce(jnp.maximum, parts, dmax[...])
    weights = [jnp.exp(part - peak) for part in parts]
    draft_weight = jnp.exp(dmax[...] - peak)
    total = draft_weight * dsum[...] + sum(
        wt * pltpu.roll(part, DIM - LINES, 1) for wt, part in zip(weights, parts)
    )
    scale = 1.0 / total
    weights = [wt * scale for wt in weights]
    draft_weight = draft_weight * scale
    for tile in range(TILES):
        first, second = tile_lines(tile)
        acc[tile] = spread(draft_weight, tile) * jnp.concatenate(
            [
                dval[pl.ds(first, REQ, stride=LINES), :],
                dval[pl.ds(second, REQ, stride=LINES), :],
            ],
            axis=0,
        )
    for tile in range(TILES):
        half, g = tile // HEADS, tile % HEADS
        line = acc[tile] + sum(
            spread(weights[m], tile) * fpay[half, m, g].astype(F32) for m in range(4)
        )
        att[half * 16 : (half + 1) * 16, g * DIM : (g + 1) * DIM] = line.astype(BF16)

    migrate_batch(5)

    w_load.wait()

    def project(k):
        columns = pl.ds(pl.multiple_of(lax.rem(tp + k, TPS) * COLS, COLS), COLS)
        return jnp.dot(att[...], w[:, columns], preferred_element_type=F32)

    def send_columns(k):
        return remote(
            zsend.at[k], zrecv.at[k], z_s.at[k], z_r.at[k], me, lax.rem(tp + k, TPS)
        )

    for k in (4, 3, 5, 2, 6, 1, 7):
        zsend[k] = project(k).astype(BF16)
        send_columns(k).start()

    zout[...] = project(0)

    for k in (1, 7, 2, 6, 3, 5, 4):
        send_columns(k).wait_recv()
        zout[...] += zrecv[k].astype(F32)

    for t in range(DRAFTS):
        for c in range(COLS // DIM):
            dval[pl.ds(c * 32 + t, REQ, stride=DRAFTS), :] = zout[
                t * REQ : (t + 1) * REQ, c * DIM : (c + 1) * DIM
            ]
    for c in range(COLS // DIM):
        out[:, c * DIM : (c + 1) * DIM] = dval[c * 32 : (c + 1) * 32, :].astype(BF16)

    for a in range(4):
        for b in range(4):
            for h in range(2):
                if (a, b) != (0, 0):
                    gather(a, b, h).wait_send()
                gather_on(a, b, h).wait_send()
    own.wait()
    for half in range(2):
        for m in range(4):
            for k in range(1, 4):
                first_pay(half, m, k).wait_send()
            if m != 0:
                second_pay(half, m).wait_send()
    for k in range(1, TPS):
        send_columns(k).wait_send()
    @pl.loop(1, INSTS)
    def _(i):
        migrate(i).wait()


def finish(out_hbm, moved_hbm, out, moved, out_held, held, in_sem, out_sem):
    size = SLOTS // PARTS

    def pair(i):
        if i == PARTS:
            return (
                pltpu.make_async_copy(out_hbm, out_held, in_sem.at[i]),
                pltpu.make_async_copy(out_held, out, out_sem.at[i]),
            )
        part = pl.ds(i * size, size)
        return (
            pltpu.make_async_copy(moved_hbm.at[part], held.at[part], in_sem.at[i]),
            pltpu.make_async_copy(held.at[part], moved.at[part], out_sem.at[i]),
        )

    pairs = [pair(i) for i in range(PARTS + 1)]
    for load, _ in pairs:
        load.start()
    for load, store in pairs:
        load.wait()
        store.start()
    for _, store in pairs:
        store.wait()


def shards(queries, new_kv, kv_cache, block_owner, block_fill, move_slot, move_target, out_weight):
    vmem = pl.BlockSpec(memory_space=pltpu.VMEM)
    anywhere = pl.BlockSpec(memory_space=pl.ANY)
    dma = pltpu.SemaphoreType.DMA
    out, moved = pl.pallas_call(
        kernel,
        out_shape=(
            jax.ShapeDtypeStruct((DRAFTS * REQ, COLS), BF16),
            jax.ShapeDtypeStruct((SLOTS, 2, ROWS, DIM), BF16),
        ),
        in_specs=[anywhere] * 8,
        out_specs=(vmem, anywhere),
        scratch_shapes=[
            pltpu.VMEM((REQ, LINES, DIM), BF16),
            pltpu.VMEM((REQ, 2, DRAFTS, DIM), BF16),
            pltpu.VMEM((SLOTS + 1, 2, ROWS, DIM), BF16),
            pltpu.VMEM((HEADS * DIM, TPS * COLS), BF16),
            pltpu.SMEM((SLOTS,), I32),
            pltpu.SMEM((SLOTS,), I32),
            pltpu.SMEM((MOVES,), I32),
            pltpu.SMEM((MOVES,), I32),
            pltpu.VMEM((8, DIM), I32),
            pltpu.SMEM((8, DIM), I32),
            pltpu.VMEM((SLOTS, 2, ROWS, DIM), BF16),
            pltpu.VMEM((INSTS * 2, REQ // 2, LINES, DIM), BF16),
            pltpu.VMEM((REQ, 2, 8, DIM), F32),
            pltpu.VMEM((REQ * LINES, DIM), F32),
            pltpu.VMEM((REQ, DIM), F32),
            pltpu.VMEM((REQ, DIM), F32),
            pltpu.VMEM((GROUPS, ROWS, DIM), F32),
            pltpu.VMEM((GROUPS, DIM), F32),
            pltpu.VMEM((GROUPS, DIM), F32),
            pltpu.VMEM((REQS, DIM), F32),
            pltpu.VMEM((REQS, DIM), F32),
            pltpu.VMEM((SLOTS * LINES, DIM), F32),
            pltpu.VMEM((2, 2, CHIPS, HEADS, 16, DIM), BF16),
            pltpu.VMEM((2, CHIPS, REQ, DIM), F32),
            pltpu.VMEM((2, CHIPS, HEADS, 16, DIM), BF16),
            pltpu.VMEM((CHIPS, REQ, DIM), F32),
            pltpu.VMEM((2, 4, 4, HEADS + 1, 16, DIM), BF16),
            pltpu.VMEM((2, 4, 4, HEADS + 1, 16, DIM), BF16),
            pltpu.VMEM((2, 4, HEADS + 1, 16, DIM), BF16),
            pltpu.VMEM((2, 4, HEADS + 1, 16, DIM), BF16),
            pltpu.VMEM((TILES, 16, DIM), F32),
            pltpu.VMEM((DRAFTS * REQ, HEADS * DIM), BF16),
            pltpu.VMEM((TPS, DRAFTS * REQ, COLS), BF16),
            pltpu.VMEM((TPS, DRAFTS * REQ, COLS), BF16),
            pltpu.VMEM((DRAFTS * REQ, COLS), F32),
            dma((9,)), dma,
            dma((2 * CHIPS,)), dma((2 * CHIPS,)), dma((2 * CHIPS,)), dma((2 * CHIPS,)),
            dma((INSTS,)), dma((INSTS,)), dma((3,)), dma((3,)),
            dma((32,)), dma((32,)), dma((8,)), dma((8,)),
            dma((TPS,)), dma((TPS,)),
        ],
        compiler_params=pltpu.CompilerParams(
            collective_id=0, has_side_effects=True, vmem_limit_bytes=63 << 20
        ),
        name="decode",
    )(
        queries.reshape(REQ, LINES, DIM),
        new_kv.reshape(REQ, 2, DRAFTS, DIM),
        kv_cache.reshape(SLOTS, 2, ROWS, DIM),
        block_owner,
        block_fill,
        move_slot,
        move_target.reshape(MOVES),
        out_weight,
    )
    out, moved = pl.pallas_call(
        finish,
        out_shape=(
            jax.ShapeDtypeStruct(out.shape, BF16),
            jax.ShapeDtypeStruct(moved.shape, BF16),
        ),
        in_specs=[anywhere] * 2,
        out_specs=(anywhere,) * 2,
        scratch_shapes=[
            pltpu.VMEM(out.shape, BF16),
            pltpu.VMEM(moved.shape, BF16),
            dma((PARTS + 1,)),
            dma((PARTS + 1,)),
        ],
        compiler_params=pltpu.CompilerParams(vmem_limit_bytes=63 << 20),
        name="finish",
    )(out, moved)
    return out, moved.reshape(kv_cache.shape)


def solution(mesh):
    placed = (
        P("inst", None, "tp", None),
        P("inst", None, None, "tp", None),
        P("inst", None, "tp", None, None),
        P("inst"),
        P("inst"),
        P("inst"),
        P("inst", None),
        P("tp", None),
    )
    return jax.shard_map(
        shards,
        mesh=mesh,
        in_specs=placed,
        out_specs=(P("inst", "tp"), P("inst", None, "tp", None, None)),
        check_vma=False,
    )
```

```python
import functools

import jax
import jax.numpy as jnp
from jax import lax
from jax.experimental import pallas as pl
from jax.experimental.pallas import tpu as pltpu
from jax.sharding import PartitionSpec as P

MESH = pl.DeviceIdType.MESH
MASKED = -1e30
CAPACITY = 2
F32, BF16, I32 = jnp.float32, jnp.bfloat16, jnp.int32

INSTS = 32
CHIPS = 16
TPS = 8
SLOTS = 64
ROWS = 64
DIM = 128
HEADS = 8
DRAFTS = 4
LINES = DRAFTS * HEADS
REQ = 8
REQS = INSTS * REQ
GROUPS = SLOTS // 4
TILES = LINES // 2
COLS = 512
MOVES = 24
BATCHES = (8, 10, 2, 0, 8)
MULT = 27
WIDE = 4
PARTS = 8
SUMS = 4


def nt_dot(a, b):
    return lax.dot_general(a, b, (((1,), (1,)), ((), ())), preferred_element_type=F32)


def tile_lines(tile):
    t, g = 2 * (tile // HEADS), tile % HEADS
    return t * HEADS + g, (t + 1) * HEADS + g


def spread(weights, tile):
    first, second = tile_lines(tile)
    return jnp.concatenate(
        [
            jnp.broadcast_to(weights[:, first : first + 1], (REQ, DIM)),
            jnp.broadcast_to(weights[:, second : second + 1], (REQ, DIM)),
        ],
        axis=0,
    )


def kernel(
    q_hbm, nkv_hbm, kv_hbm, owner_hbm, fill_hbm, slot_hbm, target_hbm, w_hbm,
    out, moved,
    q, nkv, kv, w, owner, fill, slot, target, pick, pick_s, msend, qall, dkv, dval, dmax, dsum,
    score, smax, ssum, reqmax, reqsum, val, pay, aux, epay, eaux, cpay,
    rpay, spay, fpay, acc, att, zsend, zrecv, zout,
    load_sem, own_sem, ag_s, ag_r, sib_s, sib_r, mig_s, mig_r, e_s, e_r,
    p_s, p_r, fp_s, fp_r, z_s, z_r,
):
    me, tp = lax.axis_index("inst"), lax.axis_index("tp")
    core = lax.rem(me, 2)
    chip = me // 2
    sibling = me ^ 1

    def remote(src, dst, send, recv, inst, z):
        return pltpu.make_async_remote_copy(
            src_ref=src, dst_ref=dst, send_sem=send, recv_sem=recv,
            device_id=(inst, z), device_id_type=MESH,
        )

    barrier = pltpu.get_barrier_semaphore()

    @pl.loop(1, INSTS)
    def _(k):
        pl.semaphore_signal(barrier, inc=1, device_id=(me ^ k, tp), device_id_type=MESH)

    @pl.loop(1, TPS)
    def _(k):
        pl.semaphore_signal(barrier, inc=1, device_id=(me, tp ^ k), device_id_type=MESH)

    loads = [
        pltpu.make_async_copy(src, dst, load_sem.at[i])
        for i, (src, dst) in enumerate(
            [
                (q_hbm, q),
                (slot_hbm, slot),
                (target_hbm, target),
                (nkv_hbm, nkv),
                (owner_hbm, owner),
                (fill_hbm, fill),
                (kv_hbm, kv.at[pl.ds(0, SLOTS)]),
                (w_hbm, w),
                (pick, pick_s),
            ]
        )
    ]
    q_load, slot_load, target_load, nkv_load, owner_load, fill_load, kv_load, w_load, pick_load = loads
    for load in loads[:-1]:
        load.start()

    lane = lax.broadcasted_iota(I32, (1, DIM), 1)
    lane_group = lane // LINES

    def by_group(parts):
        return jnp.where(
            lane_group == 0,
            parts[0],
            jnp.where(lane_group == 1, parts[1], jnp.where(lane_group == 2, parts[2], parts[3])),
        )

    kv[SLOTS] = jnp.zeros((2, ROWS, DIM), BF16)
    dkv[...] = jnp.zeros(dkv.shape, F32)
    slot_load.wait()
    target_load.wait()
    pick_first = jnp.full((1, DIM), SLOTS, I32)
    pick_second = pick_first
    for j in range(MOVES):
        hit = lane == target[j]
        again = hit & (pick_first != SLOTS)
        pick_second = jnp.where(again, slot[j], pick_second)
        pick_first = jnp.where(hit & (pick_first == SLOTS), slot[j], pick_first)
    pick[...] = jnp.concatenate([pick_first, pick_second] * 4, axis=0)
    pick_load.start()

    def drafts():
        dkv[:, :, 0:DRAFTS, :] = nkv[...].astype(F32)
        for half in range(REQ // 4):
            queries = q[4 * half : 4 * half + 4].reshape(4 * LINES, DIM)
            keys = dkv[4 * half : 4 * half + 4, 0].reshape(4 * 8, DIM).astype(BF16)
            full = nt_dot(keys, queries)
            scores = by_group([full[8 * i : 8 * i + 8] for i in range(4)]) * (DIM**-0.5)
            u = lax.broadcasted_iota(I32, (8, DIM), 0)
            t = lax.rem(lax.broadcasted_iota(I32, (8, DIM), 1), LINES) // HEADS
            causal = u <= t
            high = jnp.max(jnp.where(causal, scores, MASKED), axis=0, keepdims=True)
            probs = jnp.where(causal, jnp.exp(scores - high), 0.0)
            total = jnp.sum(probs, axis=0, keepdims=True)
            turned = jnp.transpose(probs).astype(BF16)
            for i in range(4):
                r = 4 * half + i
                dmax[r : r + 1, :] = high if i == 0 else pltpu.roll(high, DIM - i * LINES, 1)
                dsum[r : r + 1, :] = total if i == 0 else pltpu.roll(total, DIM - i * LINES, 1)
                dval[r * LINES : (r + 1) * LINES, :] = jnp.dot(
                    turned[i * LINES : (i + 1) * LINES],
                    dkv[r, 1].astype(BF16),
                    preferred_element_type=F32,
                )

    q_load.wait()
    qall[pl.ds(me * 2, 2)] = q[...].reshape(2, REQ // 2, LINES, DIM)

    def chunk(kx, ky, h):
        return qall.at[(me ^ (kx * 8 + ky * 2)) * 2 + h]

    def gather(kx, ky, h):
        first, on = ((kx * 8, ky * 2), (ky * 2, kx * 8))[h]
        if on == 0:
            src, to = chunk(0, 0, h), me ^ first
        else:
            src, to = (chunk(kx, 0, h), chunk(0, ky, h))[h], me ^ on
        at = h * CHIPS + kx * 4 + ky
        return remote(src, src, ag_s.at[at], ag_r.at[at], to, tp)

    def arrived(kx, ky, h):
        at = h * CHIPS + kx * 4 + ky
        ref = chunk(kx, ky, h)
        return remote(ref, ref, ag_s.at[at], ag_r.at[at], sibling, tp)

    def gather_on(kx, ky, h):
        at = h * CHIPS + kx * 4 + ky
        ref = chunk(kx, ky, h)
        return remote(ref, ref, sib_s.at[at], sib_r.at[at], sibling, tp)

    def migrate(i):
        k = lax.rem(i * MULT, INSTS)
        return remote(
            msend.at[pl.ds(CAPACITY * (me ^ k), CAPACITY)],
            moved.at[pl.ds(CAPACITY * me, CAPACITY)],
            mig_s.at[k], mig_r.at[k], me ^ k, tp,
        )

    bounds = [1 + sum(BATCHES[:i]) for i in range(len(BATCHES) + 1)] + [INSTS]

    def migrate_batch(i):
        pl.loop(bounds[i], bounds[i + 1])(lambda k: migrate(k).start())

    order = (1, 3, 2)
    nkv_load.wait()
    drafts()

    kv_load.wait()
    pick_load.wait()

    @pl.loop(0, INSTS)
    def _(d):
        for i in range(CAPACITY):
            msend[CAPACITY * d + i] = kv[pick_s[i, d]]

    pl.semaphore_wait(barrier, INSTS - 1 + TPS - 1)
    for k in (2, 1, 3):
        gather(k, 0, 0).start()
        gather(0, k, 1).start()
    for k in (2, 1, 3):
        gather(0, k, 0).start()
        gather(k, 0, 1).start()
    gather_on(0, 0, 0).start()
    gather_on(0, 0, 1).start()
    for a in order:
        arrived(a, 0, 0).wait_recv()
        for b in (2, 1, 3):
            gather(a, b, 0).start()
        arrived(0, a, 1).wait_recv()
        for b in (2, 1, 3):
            gather(b, a, 1).start()
        gather_on(a, 0, 0).start()
        gather_on(0, a, 1).start()

    migrate_batch(0)

    for a in (0,) + order:
        for b in order:
            arrived(a, b, 0).wait_recv()
            gather_on(a, b, 0).start()
            arrived(b, a, 1).wait_recv()
            gather_on(b, a, 1).start()

    own = pltpu.make_async_copy(
        msend.at[pl.ds(CAPACITY * me, CAPACITY)],
        moved.at[pl.ds(CAPACITY * me, CAPACITY)],
        own_sem,
    )
    own.start()

    migrate_batch(1)
    owner_load.wait()
    fill_load.wait()
    for a in range(4):
        for b in range(4):
            for h in range(2):
                gather_on(a, b, h).wait_recv()

    row_of = lax.broadcasted_iota(I32, (ROWS, DIM), 0)

    def usable(g):
        return row_of < by_group([fill[4 * g + i] for i in range(4)])

    def score_group(g):
        queries = jnp.concatenate(
            [qall[owner[4 * g + i] // 4, lax.rem(owner[4 * g + i], 4)] for i in range(4)], axis=0
        )
        keys = kv[pl.ds(4 * g, 4), 0].reshape(4 * ROWS, DIM)
        full = nt_dot(keys, queries)
        scores = by_group([full[ROWS * i : ROWS * (i + 1)] for i in range(4)]) * (DIM**-0.5)
        scores = jnp.where(usable(g), scores, MASKED)
        return scores, jnp.max(scores, axis=0, keepdims=True)

    row = lax.broadcasted_iota(I32, (REQS, DIM), 0)
    request = (row % (REQS // 2)) // REQ * (2 * REQ) + row // (REQS // 2) * REQ + row % REQ

    def owners(g):
        return by_group([owner[4 * g + i] for i in range(4)])

    def all_groups(x, f):
        x = f(x, pltpu.roll(x, 2 * LINES, 1))
        return f(x, pltpu.roll(x, LINES, 1))

    def weigh_group(g, scores):
        highs = []
        for i in range(4):
            o = owner[4 * g + i]
            at = lax.rem(o // REQ, 2) * (REQS // 2) + o // (2 * REQ) * REQ + lax.rem(o, REQ)
            highs.append(reqmax[pl.ds(at, 1), :])
        probs = jnp.where(usable(g), jnp.exp(scores - by_group(highs)), 0.0)
        turned = jnp.transpose(probs).astype(BF16)
        return jnp.sum(probs, axis=0, keepdims=True), [
            jnp.dot(
                turned[i * LINES : (i + 1) * LINES],
                kv[4 * g + i, 1],
                preferred_element_type=F32,
            )
            for i in range(4)
        ]

    @pl.loop(0, GROUPS // WIDE)
    def _(s):
        for g in [s * WIDE + i for i in range(WIDE)]:
            score[g], smax[pl.ds(g, 1), :] = score_group(g)

    reqmax[...] = jnp.full(reqmax.shape, MASKED, F32)

    @pl.loop(0, GROUPS // 4)
    def _(s):
        high = reqmax[...]
        for g in [s * 4 + i for i in range(4)]:
            high = jnp.where(
                request == owners(g), jnp.maximum(high, smax[pl.ds(g, 1), :]), high
            )
        reqmax[...] = high

    reqmax[...] = all_groups(reqmax[...], jnp.maximum)

    @pl.loop(0, GROUPS // WIDE)
    def _(s):
        groups = [s * WIDE + i for i in range(WIDE)]
        done = [weigh_group(g, score[g]) for g in groups]
        for g, (total, values) in zip(groups, done):
            ssum[pl.ds(g, 1), :] = total
            for i in range(4):
                val[pl.ds((4 * g + i) * LINES, LINES), :] = values[i]

    owner_lane = lax.broadcasted_iota(I32, (1, SLOTS), 1)

    def owner_step(b, x):
        return jnp.where(owner_lane == b, owner[b], x)

    half_row = lax.broadcasted_iota(I32, (REQS // 2, SLOTS), 0)

    def sum_slots(home_core, half, owner_row):
        ids = half_row // REQ * (2 * REQ) + home_core * REQ + half_row % REQ
        member = (ids == owner_row).astype(F32).astype(BF16)

        @pl.loop(0, HEADS // SUMS)
        def _(s):
            done = []
            for g in [s * SUMS + i for i in range(SUMS)]:
                first = 2 * HEADS * half + g
                lines = jnp.concatenate(
                    [
                        val[pl.ds(first, SLOTS, stride=LINES), :],
                        val[pl.ds(first + HEADS, SLOTS, stride=LINES), :],
                    ],
                    axis=1,
                ).astype(BF16)
                done.append((g, jnp.dot(member, lines, preferred_element_type=F32)))
            for g, summed in done:
                for c in range(CHIPS):
                    both = summed[c * REQ : (c + 1) * REQ]
                    pay[home_core, half, c, g] = jnp.concatenate(
                        [both[:, :DIM], both[:, DIM:]], axis=0
                    ).astype(BF16)

    def join_cores(half):
        return remote(pay.at[1 - core, half], epay.at[half], e_s.at[half], e_r.at[half], sibling, tp)

    aux_join = remote(aux.at[1 - core], eaux, e_s.at[2], e_r.at[2], sibling, tp)

    def to_parts(x):
        high = x.astype(BF16).astype(F32)
        rest = x - high
        mid = rest.astype(BF16).astype(F32)
        top = jnp.where(lane < 2 * LINES, high, pltpu.roll(mid, 2 * LINES, 1))
        return jnp.concatenate([top, rest - mid], axis=0).astype(BF16)

    def from_parts(tile):
        tile = tile.astype(F32)
        top, low = tile[:REQ], tile[REQ:]
        return (top + pltpu.roll(top, 2 * LINES, 1)) + low

    def join(half, k, m, into):
        home = chip ^ (k * 4 + m if half == 0 else m * 4 + k)
        a, b = aux[core, home], eaux[home]
        high = jnp.maximum(a, b)
        wa, wb = jnp.exp(a - high), jnp.exp(b - high)
        total = pltpu.roll(wa, LINES, 1) * a + pltpu.roll(wb, LINES, 1) * b
        into[half, m, k, HEADS] = to_parts(jnp.where(lane < LINES, high, total))
        for g in range(HEADS):
            tile = half * HEADS + g
            into[half, m, k, g] = (
                spread(wa, tile) * pay[core, half, home, g].astype(F32)
                + spread(wb, tile) * epay[half, home, g].astype(F32)
            ).astype(BF16)

    def step_of(half, k):
        return me ^ (k * 8 if half == 0 else k * 2)

    def first_pay(half, m, k):
        at = (half * 4 + m) * 4 + k
        return remote(
            cpay.at[half, m, k], rpay.at[half, m, k], p_s.at[at], p_r.at[at], step_of(half, k), tp
        )

    def second_pay(half, m):
        at = half * 4 + m
        return remote(
            spay.at[half, m], fpay.at[half, m], fp_s.at[at], fp_r.at[at], step_of(1 - half, m), tp
        )

    def merge(half, m, into):
        parts = [from_parts(rpay[half, m, k, HEADS]) for k in range(4)]
        high = functools.reduce(jnp.maximum, parts)
        weights = [jnp.exp(part - high) for part in parts]
        total = sum(pltpu.roll(wt, LINES, 1) * part for wt, part in zip(weights, parts))
        into[half, m, HEADS] = to_parts(jnp.where(lane < LINES, high, total))
        for g in range(HEADS):
            tile = half * HEADS + g
            into[half, m, g] = sum(
                spread(weights[k], tile) * rpay[half, m, k, g].astype(F32) for k in range(4)
            ).astype(BF16)

    owner_row = lax.fori_loop(0, SLOTS, owner_step, jnp.zeros((1, SLOTS), I32))
    for half in range(2):
        sum_slots(1 - core, half, owner_row)
        join_cores(half).start()
    migrate_batch(2)

    reqsum[...] = jnp.zeros(reqsum.shape, F32)

    @pl.loop(0, GROUPS // 4)
    def _(s):
        total = reqsum[...]
        for g in [s * 4 + i for i in range(4)]:
            total += jnp.where(request == owners(g), ssum[pl.ds(g, 1), :], 0.0)
        reqsum[...] = total

    reqsum[...] = all_groups(reqsum[...], jnp.add)
    aux[...] = jnp.where(lane < LINES, reqmax[...], reqsum[...]).reshape(aux.shape)
    aux_join.start()
    for half in range(2):
        sum_slots(core, half, owner_row)
    aux_join.wait()
    join_cores(0).wait()

    for m in (2, 1, 3, 0):
        for half in range(2):
            if m == 2 and half == 1:
                join_cores(1).wait()

            @pl.loop(1, 4)
            def _(k):
                join(half, k, m, cpay)
                first_pay(half, m, k).start()

        if m == 1:
            migrate_batch(3)

    for half in range(2):
        pl.loop(0, 4)(lambda m: join(half, 0, m, rpay))

    for m in (2, 1, 3, 0):
        for half in range(2):
            for k in (1, 3, 2):
                first_pay(half, m, k).wait_recv()
            merge(half, m, fpay if m == 0 else spay)
            if m != 0:
                second_pay(half, m).start()
    migrate_batch(4)

    for half in range(2):
        for m in (1, 3, 2):
            second_pay(half, m).wait_recv()

    parts = [
        jnp.where(
            lane % LINES < LINES // 2,
            from_parts(fpay[0, m, HEADS]),
            from_parts(fpay[1, m, HEADS]),
        )
        for m in range(4)
    ]
    peak = functools.reduce(jnp.maximum, parts, dmax[...])
    weights = [jnp.exp(part - peak) for part in parts]
    draft_weight = jnp.exp(dmax[...] - peak)
    total = draft_weight * dsum[...] + sum(
        wt * pltpu.roll(part, DIM - LINES, 1) for wt, part in zip(weights, parts)
    )
    scale = 1.0 / total
    weights = [wt * scale for wt in weights]
    draft_weight = draft_weight * scale
    for tile in range(TILES):
        first, second = tile_lines(tile)
        acc[tile] = spread(draft_weight, tile) * jnp.concatenate(
            [
                dval[pl.ds(first, REQ, stride=LINES), :],
                dval[pl.ds(second, REQ, stride=LINES), :],
            ],
            axis=0,
        )
    for tile in range(TILES):
        half, g = tile // HEADS, tile % HEADS
        line = acc[tile] + sum(
            spread(weights[m], tile) * fpay[half, m, g].astype(F32) for m in range(4)
        )
        att[half * 16 : (half + 1) * 16, g * DIM : (g + 1) * DIM] = line.astype(BF16)

    migrate_batch(5)

    w_load.wait()

    def project(k):
        columns = pl.ds(pl.multiple_of(lax.rem(tp + k, TPS) * COLS, COLS), COLS)
        return jnp.dot(att[...], w[:, columns], preferred_element_type=F32)

    def send_columns(k):
        return remote(
            zsend.at[k], zrecv.at[k], z_s.at[k], z_r.at[k], me, lax.rem(tp + k, TPS)
        )

    for k in (4, 3, 5, 2, 6, 1, 7):
        zsend[k] = project(k).astype(BF16)
        send_columns(k).start()

    zout[...] = project(0)

    for k in (1, 7, 2, 6, 3, 5, 4):
        send_columns(k).wait_recv()
        zout[...] += zrecv[k].astype(F32)

    for t in range(DRAFTS):
        for c in range(COLS // DIM):
            dval[pl.ds(c * 32 + t, REQ, stride=DRAFTS), :] = zout[
                t * REQ : (t + 1) * REQ, c * DIM : (c + 1) * DIM
            ]
    for c in range(COLS // DIM):
        out[:, c * DIM : (c + 1) * DIM] = dval[c * 32 : (c + 1) * 32, :].astype(BF16)

    for a in range(4):
        for b in range(4):
            for h in range(2):
                if (a, b) != (0, 0):
                    gather(a, b, h).wait_send()
                gather_on(a, b, h).wait_send()
    own.wait()
    for half in range(2):
        for m in range(4):
            for k in range(1, 4):
                first_pay(half, m, k).wait_send()
            if m != 0:
                second_pay(half, m).wait_send()
    for k in range(1, TPS):
        send_columns(k).wait_send()
    @pl.loop(1, INSTS)
    def _(i):
        migrate(i).wait()


def finish(out_hbm, moved_hbm, out, moved, out_held, held, in_sem, out_sem):
    size = SLOTS // PARTS

    def pair(i):
        if i == PARTS:
            return (
                pltpu.make_async_copy(out_hbm, out_held, in_sem.at[i]),
                pltpu.make_async_copy(out_held, out, out_sem.at[i]),
            )
        part = pl.ds(i * size, size)
        return (
            pltpu.make_async_copy(moved_hbm.at[part], held.at[part], in_sem.at[i]),
            pltpu.make_async_copy(held.at[part], moved.at[part], out_sem.at[i]),
        )

    pairs = [pair(i) for i in range(PARTS + 1)]
    for load, _ in pairs:
        load.start()
    for load, store in pairs:
        load.wait()
        store.start()
    for _, store in pairs:
        store.wait()


def shards(queries, new_kv, kv_cache, block_owner, block_fill, move_slot, move_target, out_weight):
    vmem = pl.BlockSpec(memory_space=pltpu.VMEM)
    anywhere = pl.BlockSpec(memory_space=pl.ANY)
    dma = pltpu.SemaphoreType.DMA
    out, moved = pl.pallas_call(
        kernel,
        out_shape=(
            jax.ShapeDtypeStruct((DRAFTS * REQ, COLS), BF16),
            jax.ShapeDtypeStruct((SLOTS, 2, ROWS, DIM), BF16),
        ),
        in_specs=[anywhere] * 8,
        out_specs=(vmem, anywhere),
        scratch_shapes=[
            pltpu.VMEM((REQ, LINES, DIM), BF16),
            pltpu.VMEM((REQ, 2, DRAFTS, DIM), BF16),
            pltpu.VMEM((SLOTS + 1, 2, ROWS, DIM), BF16),
            pltpu.VMEM((HEADS * DIM, TPS * COLS), BF16),
            pltpu.SMEM((SLOTS,), I32),
            pltpu.SMEM((SLOTS,), I32),
            pltpu.SMEM((MOVES,), I32),
            pltpu.SMEM((MOVES,), I32),
            pltpu.VMEM((8, DIM), I32),
            pltpu.SMEM((8, DIM), I32),
            pltpu.VMEM((SLOTS, 2, ROWS, DIM), BF16),
            pltpu.VMEM((INSTS * 2, REQ // 2, LINES, DIM), BF16),
            pltpu.VMEM((REQ, 2, 8, DIM), F32),
            pltpu.VMEM((REQ * LINES, DIM), F32),
            pltpu.VMEM((REQ, DIM), F32),
            pltpu.VMEM((REQ, DIM), F32),
            pltpu.VMEM((GROUPS, ROWS, DIM), F32),
            pltpu.VMEM((GROUPS, DIM), F32),
            pltpu.VMEM((GROUPS, DIM), F32),
            pltpu.VMEM((REQS, DIM), F32),
            pltpu.VMEM((REQS, DIM), F32),
            pltpu.VMEM((SLOTS * LINES, DIM), F32),
            pltpu.VMEM((2, 2, CHIPS, HEADS, 16, DIM), BF16),
            pltpu.VMEM((2, CHIPS, REQ, DIM), F32),
            pltpu.VMEM((2, CHIPS, HEADS, 16, DIM), BF16),
            pltpu.VMEM((CHIPS, REQ, DIM), F32),
            pltpu.VMEM((2, 4, 4, HEADS + 1, 16, DIM), BF16),
            pltpu.VMEM((2, 4, 4, HEADS + 1, 16, DIM), BF16),
            pltpu.VMEM((2, 4, HEADS + 1, 16, DIM), BF16),
            pltpu.VMEM((2, 4, HEADS + 1, 16, DIM), BF16),
            pltpu.VMEM((TILES, 16, DIM), F32),
            pltpu.VMEM((DRAFTS * REQ, HEADS * DIM), BF16),
            pltpu.VMEM((TPS, DRAFTS * REQ, COLS), BF16),
            pltpu.VMEM((TPS, DRAFTS * REQ, COLS), BF16),
            pltpu.VMEM((DRAFTS * REQ, COLS), F32),
            dma((9,)), dma,
            dma((2 * CHIPS,)), dma((2 * CHIPS,)), dma((2 * CHIPS,)), dma((2 * CHIPS,)),
            dma((INSTS,)), dma((INSTS,)), dma((3,)), dma((3,)),
            dma((32,)), dma((32,)), dma((8,)), dma((8,)),
            dma((TPS,)), dma((TPS,)),
        ],
        compiler_params=pltpu.CompilerParams(
            collective_id=0, has_side_effects=True, vmem_limit_bytes=63 << 20
        ),
        name="decode",
    )(
        queries.reshape(REQ, LINES, DIM),
        new_kv.reshape(REQ, 2, DRAFTS, DIM),
        kv_cache.reshape(SLOTS, 2, ROWS, DIM),
        block_owner,
        block_fill,
        move_slot,
        move_target.reshape(MOVES),
        out_weight,
    )
    out, moved = pl.pallas_call(
        finish,
        out_shape=(
            jax.ShapeDtypeStruct(out.shape, BF16),
            jax.ShapeDtypeStruct(moved.shape, BF16),
        ),
        in_specs=[anywhere] * 2,
        out_specs=(anywhere,) * 2,
        scratch_shapes=[
            pltpu.VMEM(out.shape, BF16),
            pltpu.VMEM(moved.shape, BF16),
            dma((PARTS + 1,)),
            dma((PARTS + 1,)),
        ],
        compiler_params=pltpu.CompilerParams(vmem_limit_bytes=63 << 20),
        name="finish",
    )(out, moved)
    return out, moved.reshape(kv_cache.shape)


def solution(mesh):
    placed = (
        P("inst", None, "tp", None),
        P("inst", None, None, "tp", None),
        P("inst", None, "tp", None, None),
        P("inst"),
        P("inst"),
        P("inst"),
        P("inst", None),
        P("tp", None),
    )
    return jax.shard_map(
        shards,
        mesh=mesh,
        in_specs=placed,
        out_specs=(P("inst", "tp"), P("inst", None, "tp", None, None)),
        check_vma=False,
    )
```

```python
import functools

import jax
import jax.numpy as jnp
from jax import lax
from jax.experimental import pallas as pl
from jax.experimental.pallas import tpu as pltpu
from jax.sharding import PartitionSpec as P

MESH = pl.DeviceIdType.MESH
MASKED = -1e30
CAPACITY = 2
F32, BF16, I32 = jnp.float32, jnp.bfloat16, jnp.int32

INSTS = 32
CHIPS = 16
TPS = 8
SLOTS = 64
ROWS = 64
DIM = 128
HEADS = 8
DRAFTS = 4
LINES = DRAFTS * HEADS
REQ = 8
REQS = INSTS * REQ
GROUPS = SLOTS // 4
TILES = LINES // 2
COLS = 512
MOVES = 24
BATCHES = (8, 10, 2, 0, 8)
MULT = 27
WIDE = 8
PARTS = 8
SUMS = 4


def nt_dot(a, b):
    return lax.dot_general(a, b, (((1,), (1,)), ((), ())), preferred_element_type=F32)


def tile_lines(tile):
    t, g = 2 * (tile // HEADS), tile % HEADS
    return t * HEADS + g, (t + 1) * HEADS + g


def spread(weights, tile):
    first, second = tile_lines(tile)
    return jnp.concatenate(
        [
            jnp.broadcast_to(weights[:, first : first + 1], (REQ, DIM)),
            jnp.broadcast_to(weights[:, second : second + 1], (REQ, DIM)),
        ],
        axis=0,
    )


def kernel(
    q_hbm, nkv_hbm, kv_hbm, owner_hbm, fill_hbm, slot_hbm, target_hbm, w_hbm,
    out, moved,
    q, nkv, kv, w, owner, fill, slot, target, pick, pick_s, msend, qall, dkv, dval, dmax, dsum,
    score, smax, ssum, reqmax, reqsum, val, pay, aux, epay, eaux, cpay,
    rpay, spay, fpay, acc, att, zsend, zrecv, zout,
    load_sem, own_sem, ag_s, ag_r, sib_s, sib_r, mig_s, mig_r, e_s, e_r,
    p_s, p_r, fp_s, fp_r, z_s, z_r,
):
    me, tp = lax.axis_index("inst"), lax.axis_index("tp")
    core = lax.rem(me, 2)
    chip = me // 2
    sibling = me ^ 1

    def remote(src, dst, send, recv, inst, z):
        return pltpu.make_async_remote_copy(
            src_ref=src, dst_ref=dst, send_sem=send, recv_sem=recv,
            device_id=(inst, z), device_id_type=MESH,
        )

    barrier = pltpu.get_barrier_semaphore()

    @pl.loop(1, INSTS)
    def _(k):
        pl.semaphore_signal(barrier, inc=1, device_id=(me ^ k, tp), device_id_type=MESH)

    @pl.loop(1, TPS)
    def _(k):
        pl.semaphore_signal(barrier, inc=1, device_id=(me, tp ^ k), device_id_type=MESH)

    loads = [
        pltpu.make_async_copy(src, dst, load_sem.at[i])
        for i, (src, dst) in enumerate(
            [
                (q_hbm, q),
                (slot_hbm, slot),
                (target_hbm, target),
                (nkv_hbm, nkv),
                (owner_hbm, owner),
                (fill_hbm, fill),
                (kv_hbm, kv.at[pl.ds(0, SLOTS)]),
                (w_hbm, w),
                (pick, pick_s),
            ]
        )
    ]
    q_load, slot_load, target_load, nkv_load, owner_load, fill_load, kv_load, w_load, pick_load = loads
    for load in loads[:-1]:
        load.start()

    lane = lax.broadcasted_iota(I32, (1, DIM), 1)
    lane_group = lane // LINES

    def by_group(parts):
        return jnp.where(
            lane_group == 0,
            parts[0],
            jnp.where(lane_group == 1, parts[1], jnp.where(lane_group == 2, parts[2], parts[3])),
        )

    kv[SLOTS] = jnp.zeros((2, ROWS, DIM), BF16)
    dkv[...] = jnp.zeros(dkv.shape, F32)
    slot_load.wait()
    target_load.wait()
    pick_first = jnp.full((1, DIM), SLOTS, I32)
    pick_second = pick_first
    for j in range(MOVES):
        hit = lane == target[j]
        again = hit & (pick_first != SLOTS)
        pick_second = jnp.where(again, slot[j], pick_second)
        pick_first = jnp.where(hit & (pick_first == SLOTS), slot[j], pick_first)
    pick[...] = jnp.concatenate([pick_first, pick_second] * 4, axis=0)
    pick_load.start()

    def drafts():
        dkv[:, :, 0:DRAFTS, :] = nkv[...].astype(F32)
        for half in range(REQ // 4):
            queries = q[4 * half : 4 * half + 4].reshape(4 * LINES, DIM)
            keys = dkv[4 * half : 4 * half + 4, 0].reshape(4 * 8, DIM).astype(BF16)
            full = nt_dot(keys, queries)
            scores = by_group([full[8 * i : 8 * i + 8] for i in range(4)]) * (DIM**-0.5)
            u = lax.broadcasted_iota(I32, (8, DIM), 0)
            t = lax.rem(lax.broadcasted_iota(I32, (8, DIM), 1), LINES) // HEADS
            causal = u <= t
            high = jnp.max(jnp.where(causal, scores, MASKED), axis=0, keepdims=True)
            probs = jnp.where(causal, jnp.exp(scores - high), 0.0)
            total = jnp.sum(probs, axis=0, keepdims=True)
            turned = jnp.transpose(probs).astype(BF16)
            for i in range(4):
                r = 4 * half + i
                dmax[r : r + 1, :] = high if i == 0 else pltpu.roll(high, DIM - i * LINES, 1)
                dsum[r : r + 1, :] = total if i == 0 else pltpu.roll(total, DIM - i * LINES, 1)
                dval[r * LINES : (r + 1) * LINES, :] = jnp.dot(
                    turned[i * LINES : (i + 1) * LINES],
                    dkv[r, 1].astype(BF16),
                    preferred_element_type=F32,
                )

    q_load.wait()
    qall[pl.ds(me * 2, 2)] = q[...].reshape(2, REQ // 2, LINES, DIM)

    def chunk(kx, ky, h):
        return qall.at[(me ^ (kx * 8 + ky * 2)) * 2 + h]

    def gather(kx, ky, h):
        first, on = ((kx * 8, ky * 2), (ky * 2, kx * 8))[h]
        if on == 0:
            src, to = chunk(0, 0, h), me ^ first
        else:
            src, to = (chunk(kx, 0, h), chunk(0, ky, h))[h], me ^ on
        at = h * CHIPS + kx * 4 + ky
        return remote(src, src, ag_s.at[at], ag_r.at[at], to, tp)

    def arrived(kx, ky, h):
        at = h * CHIPS + kx * 4 + ky
        ref = chunk(kx, ky, h)
        return remote(ref, ref, ag_s.at[at], ag_r.at[at], sibling, tp)

    def gather_on(kx, ky, h):
        at = h * CHIPS + kx * 4 + ky
        ref = chunk(kx, ky, h)
        return remote(ref, ref, sib_s.at[at], sib_r.at[at], sibling, tp)

    def migrate(i):
        k = lax.rem(i * MULT, INSTS)
        return remote(
            msend.at[pl.ds(CAPACITY * (me ^ k), CAPACITY)],
            moved.at[pl.ds(CAPACITY * me, CAPACITY)],
            mig_s.at[k], mig_r.at[k], me ^ k, tp,
        )

    bounds = [1 + sum(BATCHES[:i]) for i in range(len(BATCHES) + 1)] + [INSTS]

    def migrate_batch(i):
        pl.loop(bounds[i], bounds[i + 1])(lambda k: migrate(k).start())

    order = (1, 3, 2)
    nkv_load.wait()
    drafts()

    kv_load.wait()
    pick_load.wait()

    @pl.loop(0, INSTS)
    def _(d):
        for i in range(CAPACITY):
            msend[CAPACITY * d + i] = kv[pick_s[i, d]]

    pl.semaphore_wait(barrier, INSTS - 1 + TPS - 1)
    for k in (2, 1, 3):
        gather(k, 0, 0).start()
        gather(0, k, 1).start()
    for k in (2, 1, 3):
        gather(0, k, 0).start()
        gather(k, 0, 1).start()
    gather_on(0, 0, 0).start()
    gather_on(0, 0, 1).start()
    for a in order:
        arrived(a, 0, 0).wait_recv()
        for b in (2, 1, 3):
            gather(a, b, 0).start()
        arrived(0, a, 1).wait_recv()
        for b in (2, 1, 3):
            gather(b, a, 1).start()
        gather_on(a, 0, 0).start()
        gather_on(0, a, 1).start()

    migrate_batch(0)

    for a in (0,) + order:
        for b in order:
            arrived(a, b, 0).wait_recv()
            gather_on(a, b, 0).start()
            arrived(b, a, 1).wait_recv()
            gather_on(b, a, 1).start()

    own = pltpu.make_async_copy(
        msend.at[pl.ds(CAPACITY * me, CAPACITY)],
        moved.at[pl.ds(CAPACITY * me, CAPACITY)],
        own_sem,
    )
    own.start()

    migrate_batch(1)
    owner_load.wait()
    fill_load.wait()
    for a in range(4):
        for b in range(4):
            for h in range(2):
                gather_on(a, b, h).wait_recv()

    row_of = lax.broadcasted_iota(I32, (ROWS, DIM), 0)

    def usable(g):
        return row_of < by_group([fill[4 * g + i] for i in range(4)])

    def score_group(g):
        queries = jnp.concatenate(
            [qall[owner[4 * g + i] // 4, lax.rem(owner[4 * g + i], 4)] for i in range(4)], axis=0
        )
        keys = kv[pl.ds(4 * g, 4), 0].reshape(4 * ROWS, DIM)
        full = nt_dot(keys, queries)
        scores = by_group([full[ROWS * i : ROWS * (i + 1)] for i in range(4)]) * (DIM**-0.5)
        scores = jnp.where(usable(g), scores, MASKED)
        return scores, jnp.max(scores, axis=0, keepdims=True)

    row = lax.broadcasted_iota(I32, (REQS, DIM), 0)
    request = (row % (REQS // 2)) // REQ * (2 * REQ) + row // (REQS // 2) * REQ + row % REQ

    def owners(g):
        return by_group([owner[4 * g + i] for i in range(4)])

    def all_groups(x, f):
        x = f(x, pltpu.roll(x, 2 * LINES, 1))
        return f(x, pltpu.roll(x, LINES, 1))

    def weigh_group(g, scores):
        highs = []
        for i in range(4):
            o = owner[4 * g + i]
            at = lax.rem(o // REQ, 2) * (REQS // 2) + o // (2 * REQ) * REQ + lax.rem(o, REQ)
            highs.append(reqmax[pl.ds(at, 1), :])
        probs = jnp.where(usable(g), jnp.exp(scores - by_group(highs)), 0.0)
        turned = jnp.transpose(probs).astype(BF16)
        return jnp.sum(probs, axis=0, keepdims=True), [
            jnp.dot(
                turned[i * LINES : (i + 1) * LINES],
                kv[4 * g + i, 1],
                preferred_element_type=F32,
            )
            for i in range(4)
        ]

    @pl.loop(0, GROUPS // WIDE)
    def _(s):
        for g in [s * WIDE + i for i in range(WIDE)]:
            score[g], smax[pl.ds(g, 1), :] = score_group(g)

    reqmax[...] = jnp.full(reqmax.shape, MASKED, F32)

    @pl.loop(0, GROUPS // 4)
    def _(s):
        high = reqmax[...]
        for g in [s * 4 + i for i in range(4)]:
            high = jnp.where(
                request == owners(g), jnp.maximum(high, smax[pl.ds(g, 1), :]), high
            )
        reqmax[...] = high

    reqmax[...] = all_groups(reqmax[...], jnp.maximum)

    @pl.loop(0, GROUPS // WIDE)
    def _(s):
        groups = [s * WIDE + i for i in range(WIDE)]
        done = [weigh_group(g, score[g]) for g in groups]
        for g, (total, values) in zip(groups, done):
            ssum[pl.ds(g, 1), :] = total
            for i in range(4):
                val[pl.ds((4 * g + i) * LINES, LINES), :] = values[i]

    owner_lane = lax.broadcasted_iota(I32, (1, SLOTS), 1)

    def owner_step(b, x):
        return jnp.where(owner_lane == b, owner[b], x)

    half_row = lax.broadcasted_iota(I32, (REQS // 2, SLOTS), 0)

    def sum_slots(home_core, half, owner_row):
        ids = half_row // REQ * (2 * REQ) + home_core * REQ + half_row % REQ
        member = (ids == owner_row).astype(F32).astype(BF16)

        @pl.loop(0, HEADS // SUMS)
        def _(s):
            done = []
            for g in [s * SUMS + i for i in range(SUMS)]:
                first = 2 * HEADS * half + g
                lines = jnp.concatenate(
                    [
                        val[pl.ds(first, SLOTS, stride=LINES), :],
                        val[pl.ds(first + HEADS, SLOTS, stride=LINES), :],
                    ],
                    axis=1,
                ).astype(BF16)
                done.append((g, jnp.dot(member, lines, preferred_element_type=F32)))
            for g, summed in done:
                for c in range(CHIPS):
                    both = summed[c * REQ : (c + 1) * REQ]
                    pay[home_core, half, c, g] = jnp.concatenate(
                        [both[:, :DIM], both[:, DIM:]], axis=0
                    ).astype(BF16)

    def join_cores(half):
        return remote(pay.at[1 - core, half], epay.at[half], e_s.at[half], e_r.at[half], sibling, tp)

    aux_join = remote(aux.at[1 - core], eaux, e_s.at[2], e_r.at[2], sibling, tp)

    def to_parts(x):
        high = x.astype(BF16).astype(F32)
        rest = x - high
        mid = rest.astype(BF16).astype(F32)
        top = jnp.where(lane < 2 * LINES, high, pltpu.roll(mid, 2 * LINES, 1))
        return jnp.concatenate([top, rest - mid], axis=0).astype(BF16)

    def from_parts(tile):
        tile = tile.astype(F32)
        top, low = tile[:REQ], tile[REQ:]
        return (top + pltpu.roll(top, 2 * LINES, 1)) + low

    def join(half, k, m, into):
        home = chip ^ (k * 4 + m if half == 0 else m * 4 + k)
        a, b = aux[core, home], eaux[home]
        high = jnp.maximum(a, b)
        wa, wb = jnp.exp(a - high), jnp.exp(b - high)
        total = pltpu.roll(wa, LINES, 1) * a + pltpu.roll(wb, LINES, 1) * b
        into[half, m, k, HEADS] = to_parts(jnp.where(lane < LINES, high, total))
        for g in range(HEADS):
            tile = half * HEADS + g
            into[half, m, k, g] = (
                spread(wa, tile) * pay[core, half, home, g].astype(F32)
                + spread(wb, tile) * epay[half, home, g].astype(F32)
            ).astype(BF16)

    def step_of(half, k):
        return me ^ (k * 8 if half == 0 else k * 2)

    def first_pay(half, m, k):
        at = (half * 4 + m) * 4 + k
        return remote(
            cpay.at[half, m, k], rpay.at[half, m, k], p_s.at[at], p_r.at[at], step_of(half, k), tp
        )

    def second_pay(half, m):
        at = half * 4 + m
        return remote(
            spay.at[half, m], fpay.at[half, m], fp_s.at[at], fp_r.at[at], step_of(1 - half, m), tp
        )

    def merge(half, m, into):
        parts = [from_parts(rpay[half, m, k, HEADS]) for k in range(4)]
        high = functools.reduce(jnp.maximum, parts)
        weights = [jnp.exp(part - high) for part in parts]
        total = sum(pltpu.roll(wt, LINES, 1) * part for wt, part in zip(weights, parts))
        into[half, m, HEADS] = to_parts(jnp.where(lane < LINES, high, total))
        for g in range(HEADS):
            tile = half * HEADS + g
            into[half, m, g] = sum(
                spread(weights[k], tile) * rpay[half, m, k, g].astype(F32) for k in range(4)
            ).astype(BF16)

    owner_row = lax.fori_loop(0, SLOTS, owner_step, jnp.zeros((1, SLOTS), I32))
    for half in range(2):
        sum_slots(1 - core, half, owner_row)
        join_cores(half).start()
    migrate_batch(2)

    reqsum[...] = jnp.zeros(reqsum.shape, F32)

    @pl.loop(0, GROUPS // 4)
    def _(s):
        total = reqsum[...]
        for g in [s * 4 + i for i in range(4)]:
            total += jnp.where(request == owners(g), ssum[pl.ds(g, 1), :], 0.0)
        reqsum[...] = total

    reqsum[...] = all_groups(reqsum[...], jnp.add)
    aux[...] = jnp.where(lane < LINES, reqmax[...], reqsum[...]).reshape(aux.shape)
    aux_join.start()
    for half in range(2):
        sum_slots(core, half, owner_row)
    aux_join.wait()
    join_cores(0).wait()

    for m in (2, 1, 3, 0):
        for half in range(2):
            if m == 2 and half == 1:
                join_cores(1).wait()

            @pl.loop(0, 3)
            def _(i):
                k = lax.rem(i + 1, 3) + 1
                join(half, k, m, cpay)
                first_pay(half, m, k).start()

        if m == 1:
            migrate_batch(3)

    for half in range(2):
        pl.loop(0, 4)(lambda m: join(half, 0, m, rpay))

    for m in (2, 1, 3, 0):
        for half in range(2):
            for k in (1, 3, 2):
                first_pay(half, m, k).wait_recv()
            merge(half, m, fpay if m == 0 else spay)
            if m != 0:
                second_pay(half, m).start()
    migrate_batch(4)

    for half in range(2):
        for m in (1, 3, 2):
            second_pay(half, m).wait_recv()

    parts = [
        jnp.where(
            lane % LINES < LINES // 2,
            from_parts(fpay[0, m, HEADS]),
            from_parts(fpay[1, m, HEADS]),
        )
        for m in range(4)
    ]
    peak = functools.reduce(jnp.maximum, parts, dmax[...])
    weights = [jnp.exp(part - peak) for part in parts]
    draft_weight = jnp.exp(dmax[...] - peak)
    total = draft_weight * dsum[...] + sum(
        wt * pltpu.roll(part, DIM - LINES, 1) for wt, part in zip(weights, parts)
    )
    scale = 1.0 / total
    weights = [wt * scale for wt in weights]
    draft_weight = draft_weight * scale
    for tile in range(TILES):
        first, second = tile_lines(tile)
        acc[tile] = spread(draft_weight, tile) * jnp.concatenate(
            [
                dval[pl.ds(first, REQ, stride=LINES), :],
                dval[pl.ds(second, REQ, stride=LINES), :],
            ],
            axis=0,
        )
    for tile in range(TILES):
        half, g = tile // HEADS, tile % HEADS
        line = acc[tile] + sum(
            spread(weights[m], tile) * fpay[half, m, g].astype(F32) for m in range(4)
        )
        att[half * 16 : (half + 1) * 16, g * DIM : (g + 1) * DIM] = line.astype(BF16)

    migrate_batch(5)

    w_load.wait()

    def project(k):
        columns = pl.ds(pl.multiple_of(lax.rem(tp + k, TPS) * COLS, COLS), COLS)
        return jnp.dot(att[...], w[:, columns], preferred_element_type=F32)

    def send_columns(k):
        return remote(
            zsend.at[k], zrecv.at[k], z_s.at[k], z_r.at[k], me, lax.rem(tp + k, TPS)
        )

    for k in (4, 3, 5, 2, 6, 1, 7):
        zsend[k] = project(k).astype(BF16)
        send_columns(k).start()

    zout[...] = project(0)

    for k in (1, 7, 2, 6, 3, 5, 4):
        send_columns(k).wait_recv()
        zout[...] += zrecv[k].astype(F32)

    for t in range(DRAFTS):
        for c in range(COLS // DIM):
            dval[pl.ds(c * 32 + t, REQ, stride=DRAFTS), :] = zout[
                t * REQ : (t + 1) * REQ, c * DIM : (c + 1) * DIM
            ]
    for c in range(COLS // DIM):
        out[:, c * DIM : (c + 1) * DIM] = dval[c * 32 : (c + 1) * 32, :].astype(BF16)

    for a in range(4):
        for b in range(4):
            for h in range(2):
                if (a, b) != (0, 0):
                    gather(a, b, h).wait_send()
                gather_on(a, b, h).wait_send()
    own.wait()
    for half in range(2):
        for m in range(4):
            for k in range(1, 4):
                first_pay(half, m, k).wait_send()
            if m != 0:
                second_pay(half, m).wait_send()
    for k in range(1, TPS):
        send_columns(k).wait_send()
    @pl.loop(1, INSTS)
    def _(i):
        migrate(i).wait()


def finish(out_hbm, moved_hbm, out, moved, out_held, held, in_sem, out_sem):
    size = SLOTS // PARTS

    def pair(i):
        if i == PARTS:
            return (
                pltpu.make_async_copy(out_hbm, out_held, in_sem.at[i]),
                pltpu.make_async_copy(out_held, out, out_sem.at[i]),
            )
        part = pl.ds(i * size, size)
        return (
            pltpu.make_async_copy(moved_hbm.at[part], held.at[part], in_sem.at[i]),
            pltpu.make_async_copy(held.at[part], moved.at[part], out_sem.at[i]),
        )

    pairs = [pair(i) for i in range(PARTS + 1)]
    for load, _ in pairs:
        load.start()
    for load, store in pairs:
        load.wait()
        store.start()
    for _, store in pairs:
        store.wait()


def shards(queries, new_kv, kv_cache, block_owner, block_fill, move_slot, move_target, out_weight):
    vmem = pl.BlockSpec(memory_space=pltpu.VMEM)
    anywhere = pl.BlockSpec(memory_space=pl.ANY)
    dma = pltpu.SemaphoreType.DMA
    out, moved = pl.pallas_call(
        kernel,
        out_shape=(
            jax.ShapeDtypeStruct((DRAFTS * REQ, COLS), BF16),
            jax.ShapeDtypeStruct((SLOTS, 2, ROWS, DIM), BF16),
        ),
        in_specs=[anywhere] * 8,
        out_specs=(vmem, anywhere),
        scratch_shapes=[
            pltpu.VMEM((REQ, LINES, DIM), BF16),
            pltpu.VMEM((REQ, 2, DRAFTS, DIM), BF16),
            pltpu.VMEM((SLOTS + 1, 2, ROWS, DIM), BF16),
            pltpu.VMEM((HEADS * DIM, TPS * COLS), BF16),
            pltpu.SMEM((SLOTS,), I32),
            pltpu.SMEM((SLOTS,), I32),
            pltpu.SMEM((MOVES,), I32),
            pltpu.SMEM((MOVES,), I32),
            pltpu.VMEM((8, DIM), I32),
            pltpu.SMEM((8, DIM), I32),
            pltpu.VMEM((SLOTS, 2, ROWS, DIM), BF16),
            pltpu.VMEM((INSTS * 2, REQ // 2, LINES, DIM), BF16),
            pltpu.VMEM((REQ, 2, 8, DIM), F32),
            pltpu.VMEM((REQ * LINES, DIM), F32),
            pltpu.VMEM((REQ, DIM), F32),
            pltpu.VMEM((REQ, DIM), F32),
            pltpu.VMEM((GROUPS, ROWS, DIM), F32),
            pltpu.VMEM((GROUPS, DIM), F32),
            pltpu.VMEM((GROUPS, DIM), F32),
            pltpu.VMEM((REQS, DIM), F32),
            pltpu.VMEM((REQS, DIM), F32),
            pltpu.VMEM((SLOTS * LINES, DIM), F32),
            pltpu.VMEM((2, 2, CHIPS, HEADS, 16, DIM), BF16),
            pltpu.VMEM((2, CHIPS, REQ, DIM), F32),
            pltpu.VMEM((2, CHIPS, HEADS, 16, DIM), BF16),
            pltpu.VMEM((CHIPS, REQ, DIM), F32),
            pltpu.VMEM((2, 4, 4, HEADS + 1, 16, DIM), BF16),
            pltpu.VMEM((2, 4, 4, HEADS + 1, 16, DIM), BF16),
            pltpu.VMEM((2, 4, HEADS + 1, 16, DIM), BF16),
            pltpu.VMEM((2, 4, HEADS + 1, 16, DIM), BF16),
            pltpu.VMEM((TILES, 16, DIM), F32),
            pltpu.VMEM((DRAFTS * REQ, HEADS * DIM), BF16),
            pltpu.VMEM((TPS, DRAFTS * REQ, COLS), BF16),
            pltpu.VMEM((TPS, DRAFTS * REQ, COLS), BF16),
            pltpu.VMEM((DRAFTS * REQ, COLS), F32),
            dma((9,)), dma,
            dma((2 * CHIPS,)), dma((2 * CHIPS,)), dma((2 * CHIPS,)), dma((2 * CHIPS,)),
            dma((INSTS,)), dma((INSTS,)), dma((3,)), dma((3,)),
            dma((32,)), dma((32,)), dma((8,)), dma((8,)),
            dma((TPS,)), dma((TPS,)),
        ],
        compiler_params=pltpu.CompilerParams(
            collective_id=0, has_side_effects=True, vmem_limit_bytes=63 << 20
        ),
        name="decode",
    )(
        queries.reshape(REQ, LINES, DIM),
        new_kv.reshape(REQ, 2, DRAFTS, DIM),
        kv_cache.reshape(SLOTS, 2, ROWS, DIM),
        block_owner,
        block_fill,
        move_slot,
        move_target.reshape(MOVES),
        out_weight,
    )
    out, moved = pl.pallas_call(
        finish,
        out_shape=(
            jax.ShapeDtypeStruct(out.shape, BF16),
            jax.ShapeDtypeStruct(moved.shape, BF16),
        ),
        in_specs=[anywhere] * 2,
        out_specs=(anywhere,) * 2,
        scratch_shapes=[
            pltpu.VMEM(out.shape, BF16),
            pltpu.VMEM(moved.shape, BF16),
            dma((PARTS + 1,)),
            dma((PARTS + 1,)),
        ],
        compiler_params=pltpu.CompilerParams(vmem_limit_bytes=63 << 20),
        name="finish",
    )(out, moved)
    return out, moved.reshape(kv_cache.shape)


def solution(mesh):
    placed = (
        P("inst", None, "tp", None),
        P("inst", None, None, "tp", None),
        P("inst", None, "tp", None, None),
        P("inst"),
        P("inst"),
        P("inst"),
        P("inst", None),
        P("tp", None),
    )
    return jax.shard_map(
        shards,
        mesh=mesh,
        in_specs=placed,
        out_specs=(P("inst", "tp"), P("inst", None, "tp", None, None)),
        check_vma=False,
    )
```
